128 devices in a mesh: leaf: 8 (over z, core), node: 16 (over y, x).
Axes of the slice: x: 4, y: 4, z: 4, core: 2. Of those that a mesh axis runs over, the one named last changes fastest.
Arguments:
- queries: bfloat16 [16384, 5120], P(('leaf', 'node')), parts along dimension 0, may hold values from -100 to 100
- leaf_kv: bfloat16 [2, 16384, 1024], P(None, ('leaf', 'node')), parts along dimension 1, may hold values from -6 to 6
- node_kv: bfloat16 [2, 128, 1024, 1024], P(None, ('leaf', 'node')), parts along dimension 1, may hold values from -6 to 6
- node_lengths: int32 [128], P('leaf'), parts along dimension 0, may hold values from 1 to 1024, 12288 in all
- ancestors: int32 [1024, 3], P(('leaf', 'node')), parts along dimension 0, may hold values from 0 to 15, all different within a row; in each aligned block of 8 rows (0 to 7, 8 to 15, ...) at most 3 rows name the same one
Outputs:
- attended: float32 [16384, 5120], P(('leaf', 'node')), parts along dimension 0
The draws below stay inside these ranges and needn't reach their ends.
There are 8 independent parts, one for each index of `leaf`. The reference program is written for one: setup_inputs(seed, part) draws one part's arguments, and reference() takes and returns one part's arrays. A program takes and returns all parts, laid end to end along the dimension named above; each array names one. Nothing has to cross between parts.
Inputs may be any that keep to these rules, and one draw needn't show every extreme that they name: The 3 ancestors of a leaf are different nodes. Among the 8 leaves of one device no node is named more than 3 times, a bound that some block reaches. Node n is kept by device n // 1 of the tree. `node_lengths`: some node has all 1024 positions valid.
All inputs are finite; a program needn't handle non-finite values.
Results may differ from the reference program's by a relative error of at most 0.0026.
Values may be sent and summed in bfloat16 or wider, within the bound.
No kernel may reach another device: no remote copies, remote signals or barrier semaphores. Data moves between devices by JAX's collectives and lax.ppermute only.
A program may use at most 192 MiB of HBM per device.

```python
import math
import jax
import jax.numpy as jnp
import numpy as np
from jax import lax

HEADS = 40
KV_HEADS = 8
HEAD_DIM = 128
LEAVES_DEV = 8
NODE_LEN = 1024
LEAF_LEN = 16
DEPTH = 3
MOST = 3
LEAVES = 128
NODES = 16
TOKENS = 2048


def base_keys(key):
    return jnp.clip(jax.random.normal(key, (TOKENS, KV_HEADS * HEAD_DIM), jnp.float32), -5.0, 5.0)


def draw_leaf_kv(key, part):
    keys = base_keys(key)
    key = jax.random.fold_in(key, 11)
    first = jax.random.fold_in(key, 0)
    values = jnp.clip(jax.random.normal(first, keys.shape, jnp.float32), -5.0, 5.0)
    return jnp.stack([keys, values]).astype(jnp.bfloat16)


def draw_queries(key, part):
    key = jax.random.fold_in(key, 7)
    rows = jnp.clip(jax.random.normal(key, (TOKENS, HEADS * HEAD_DIM), jnp.float32), -6.0, 6.0)
    return rows.astype(jnp.bfloat16)


def levels(own_key, extent, cuts, smallest, largest):
    gain, own = 1.0, jax.random.fold_in(own_key, 6)
    for axis_at, parts in cuts:
        steps = jnp.exp(jax.random.uniform(jax.random.fold_in(own, axis_at), (parts,), jnp.float32, smallest / len(cuts), largest / len(cuts)))
        gain = gain * jnp.repeat(steps, extent[axis_at] // parts).reshape([-1 if axis == axis_at else 1 for axis in range(len(extent))])
    return gain


def length_profile(number_of, total, reach, lean):
    weights = [(1 << 20) // math.isqrt(grade ** lean) + 1 for grade in range(2, number_of + 1)]
    spare, counts = total - reach - (number_of - 1), [1] * (number_of - 1)
    while spare > 0:
        free = [i for i in range(number_of - 1) if counts[i] < reach]
        pool, budget = sum([weights[i] for i in free]), spare
        for i in free:
            more = min(reach - counts[i], max(1, budget * weights[i] // pool), spare)
            counts[i] = counts[i] + more
            spare = spare - more
    return np.array([reach] + counts)


def uneven(stream_key, amount, total, most, skew):
    if amount == 2:
        one = jax.random.randint(stream_key, (), max(1, total - most), min(most, total - 1) + 1)
        return jnp.stack([one, total - one])
    sizes = jnp.asarray(length_profile(amount, total, most, skew), jnp.int32)
    pairs = (amount - 1) // 2
    giver, taker = sizes[1:1 + 2 * pairs:2], sizes[2:2 + 2 * pairs:2]
    room = jnp.minimum(giver - 1, most - taker)
    shifted = jax.random.randint(jax.random.fold_in(stream_key, 1), (pairs,), 0, 1 << 20) % (room + 1)
    sizes = sizes.at[1:1 + 2 * pairs:2].set(giver - shifted).at[2:2 + 2 * pairs:2].set(taker + shifted)
    return sizes[jax.random.permutation(jax.random.fold_in(stream_key, 2), amount)]


def deal_out(rng, own, number, rows, amount, top, limit, skew):
    order = jax.random.permutation(rng, amount)
    heavy_load, ordinary = portions_of(amount, rows * top, limit, skew, True), portions_of(amount, rows * top, limit, skew, False)
    places = jnp.arange(amount)

    def named(lengths, turn):
        used = int((lengths > 0).sum())
        fixed = max(1, used // 4)
        passed = fixed + (places - fixed + turn * (used - fixed)) % max(1, amount - fixed)
        return jnp.zeros((amount,), jnp.int32).at[order[jnp.where(places < fixed, places, passed)]].set(jnp.asarray(lengths, jnp.int32))

    lengths = jnp.where(number % 4 == 0, named(heavy_load, number // 4), named(ordinary, number - number // 4 - 1))
    mixed = jax.random.permutation(jax.random.fold_in(own, 3), amount)
    donor, sink = mixed[0:amount // 2 * 2:2], mixed[1:amount // 2 * 2:2]
    room = jnp.minimum(lengths[donor] - 1, limit - lengths[sink]) // 2
    room = jnp.where((donor == order[0]) | (sink == order[0]) | (lengths[sink] == 0), 0, jnp.maximum(room, 0))
    passed = jax.random.randint(jax.random.fold_in(own, 4), (amount // 2,), 0, 1 << 20) % (room + 1)
    lengths = lengths.at[donor].add(-passed).at[sink].add(passed)
    items = jnp.searchsorted(jnp.cumsum(lengths), jnp.arange(rows * top), side="right").astype(jnp.int32)
    table = items.reshape(top, rows).T
    table = table[jax.random.permutation(jax.random.fold_in(own, 1), rows)]
    turn = jax.random.randint(jax.random.fold_in(own, 2), (rows, 1), 0, top)
    return jnp.take_along_axis(table, (jnp.arange(top)[None, :] + turn) % top, axis=1)


def portions_of(amount, total, bound, skew, full):
    portions = [(1 << 20) // math.isqrt(grade ** skew) + 1 for grade in range(1, amount + 1)]
    largest = bound if full else min(bound, max(-(-total // amount), total * portions[0] // sum(portions)))
    least = 1 if total - largest >= amount - 1 else 0
    counts, rest = [largest] + [least] * (amount - 1), total - largest - least * (amount - 1)
    while rest > 0:
        candidates = [i for i in range(1, amount) if counts[i] < largest] or [i for i in range(1, amount) if counts[i] < bound]
        pool, remaining = sum([portions[i] for i in candidates]), rest
        for i in candidates:
            extra = min(bound - counts[i], max(1, remaining * portions[i] // pool), rest)
            counts[i] = counts[i] + extra
            rest = rest - extra
    return np.array(counts)


def gaussian(stream_key, shape, scale, bound, cuts=(), kind=jnp.bfloat16):
    factor_of = levels(stream_key, shape, cuts, -0.22, 0.18) if cuts else 1.0
    values = jax.random.normal(stream_key, shape, jnp.float32) * scale * factor_of
    return jnp.minimum(jnp.maximum(values, -bound), bound).astype(kind)


def setup_inputs(seed: int = 0, part: int = 0) -> dict:
    splits = jax.random.split(jax.random.key(seed), 6)
    own_keys = jax.random.split(jax.random.fold_in(splits[5], part), 6)
    queries = draw_queries(jax.random.fold_in(jax.random.fold_in(splits[5], part), 71), part)
    leaf_kv = draw_leaf_kv(jax.random.fold_in(jax.random.fold_in(splits[5], part), 71), part)
    node_kv = gaussian(own_keys[2], (2, NODES, NODE_LEN, KV_HEADS * HEAD_DIM), 1.0, 6.0, ((1, 16),))
    node_lengths = uneven(own_keys[3], NODES, NODES * NODE_LEN * 3 // 4, NODE_LEN, 1).astype(jnp.int32)
    ancestors_keys = jax.random.split(jax.random.fold_in(own_keys[4], 1), LEAVES // LEAVES_DEV)
    ancestors_turns = jax.random.permutation(jax.random.fold_in(own_keys[4], 3), LEAVES // LEAVES_DEV)
    ancestors = jax.vmap(lambda own, number: deal_out(jax.random.fold_in(own_keys[4], 2), own, number, LEAVES_DEV, NODES, DEPTH, MOST, 2))(ancestors_keys, ancestors_turns).reshape((LEAVES, DEPTH))
    return dict(queries=queries, leaf_kv=leaf_kv, node_kv=node_kv, node_lengths=node_lengths, ancestors=ancestors)


def partial_attend(rows, keys, values, mask):
    count = rows.shape[0]
    group = HEADS // KV_HEADS
    query_four = rows.astype(jnp.float32).reshape(count, KV_HEADS, group, HEAD_DIM)
    key_three = keys.astype(jnp.float32).reshape(-1, KV_HEADS, HEAD_DIM)
    value_three = values.astype(jnp.float32).reshape(-1, KV_HEADS, HEAD_DIM)
    scores = jnp.einsum("rgjd,kgd->rgjk", query_four, key_three, precision=lax.Precision.HIGHEST) * (HEAD_DIM ** -0.5)
    scores = jnp.where(mask[:, None, None, :], scores, -1e30)
    top = jnp.max(scores, axis=-1, keepdims=True)
    weights = jnp.exp(scores - top)
    total = jnp.sum(weights, axis=-1)
    probs = weights.astype(jnp.bfloat16).astype(jnp.float32)
    mixed = jnp.einsum("rgjk,kgd->rgjd", probs, value_three, precision=lax.Precision.HIGHEST) / total[..., None]
    lse = top[..., 0] + jnp.log(total)
    return mixed.reshape(count, HEADS, HEAD_DIM), lse.reshape(count, HEADS)


def reference(queries, leaf_kv, node_kv, node_lengths, ancestors):
    position = jnp.arange(LEAF_LEN)
    causal = position[None, :] <= position[:, None]
    live = jnp.arange(NODE_LEN)

    def one_leaf(leaf):
        start = (leaf * LEAF_LEN).astype(jnp.int32)
        rows = lax.dynamic_slice_in_dim(queries, start, LEAF_LEN, 0)
        own = lax.dynamic_slice_in_dim(leaf_kv, start, LEAF_LEN, 1)
        self_out, self_lse = partial_attend(rows, own[0], own[1], causal)
        outs = [self_out]
        lses = [self_lse]
        for depth in range(DEPTH):
            node = ancestors[leaf, depth].astype(jnp.int32)
            cache = lax.dynamic_index_in_dim(node_kv, node, 1, keepdims=False)
            mask = jnp.broadcast_to((live < node_lengths[node])[None, :], (LEAF_LEN, NODE_LEN))
            node_out, node_lse = partial_attend(rows, cache[0], cache[1], mask)
            outs.append(node_out)
            lses.append(node_lse)
        all_out = jnp.stack(outs, 0)
        all_lse = jnp.stack(lses, 0)
        top = jnp.max(all_lse, axis=0, keepdims=True)
        whole = top + jnp.log(jnp.sum(jnp.exp(all_lse - top), axis=0, keepdims=True))
        share = jnp.exp(all_lse - whole)
        merged = jnp.sum(share[..., None] * all_out, axis=0)
        return merged.reshape(LEAF_LEN, HEADS * HEAD_DIM)

    blocks = lax.map(one_leaf, jnp.arange(ancestors.shape[0], dtype=jnp.int32))
    return blocks.reshape(ancestors.shape[0] * LEAF_LEN, HEADS * HEAD_DIM)
```

```python
import functools
import jax
import jax.numpy as jnp
from jax import lax
from jax.experimental import pallas as pl
from jax.experimental.pallas import tpu as pltpu
from jax.sharding import PartitionSpec as P

SCALE2 = (128 ** -0.5) * 1.4426950408889634
LN2 = 0.6931471805599453
SPAN = 1024
C = 4
R = 80
SHIFTS = ((0, 0), (2, 0), (1, 1), (3, 1), (0, 1), (0, 3), (1, 0), (3, 0))
COLOUR = tuple((y % 2) * 4 + (x + 2 * (y // 2)) % 4 for y in range(4) for x in range(4))
FIRST = tuple(COLOUR.index(g) for g in range(8))
SECOND = tuple(15 - COLOUR[::-1].index(g) for g in range(8))


def iota(shape, axis):
    return lax.broadcasted_iota(jnp.int32, shape, axis)


def make_lists(me, q_ref, meta, meta_smem, sem):
    named = q_ref[0, 640:656].astype(jnp.float32)
    for src in range(1, 16):
        named = named + q_ref[src, 640:656].astype(jnp.float32)
    y, x = me // 4, me % 4
    nodes = jnp.full((128, 128), -1, jnp.int32)
    for i, (dy, dx) in enumerate(SHIFTS):
        node = (y + 4 - dy) % 4 * 4 + (x + 4 - dx) % 4
        nodes = jnp.where(iota((128, 128), 0) == i, node, nodes)
    nodes = nodes.astype(jnp.float32)
    member = (nodes == named[0:1]) | (nodes == named[1:2]) | (nodes == named[2:3])
    member = jnp.where(member, 1.0, 0.0).astype(jnp.bfloat16)
    lower = jnp.where(iota((128, 128), 1) <= iota((128, 128), 0), 1.0, 0.0).astype(jnp.bfloat16)
    count = lax.dot_general(lower, member, (((1,), (1,)), ((), ())), preferred_element_type=jnp.float32)
    place = iota((128, 128), 1).astype(jnp.float32)
    for i in range(8):
        before = jnp.where(count[:, i:i + 1] <= place, 1.0, 0.0)
        meta[i:i + 1] = jnp.sum(before, axis=0, keepdims=True).astype(jnp.int32)
    meta[8:9] = count[127:128].astype(jnp.int32)
    copy = pltpu.make_async_copy(meta, meta_smem, sem)
    copy.start()
    copy.wait()


def attend_kernel(me_ref, lengths, q_ref, *refs):
    kv_in = refs[:8]
    out_ref = refs[8]
    kv, acc, top, tot, lse, meta, lists, seen, sem, meta_sem = refs[9:]
    copies = [pltpu.make_async_copy(kv_in[i], kv.at[i], sem.at[i]) for i in range(8)]
    for c in copies:
        c.start()
    me = me_ref[0]
    make_lists(me, q_ref, meta, lists, meta_sem)

    def clear(i, _):
        seen[i] = 0
        return 0
    lax.fori_loop(0, 128, clear, 0)
    for c in copies:
        c.wait()
    nodes = [(me // 4 + 4 - dy) % 4 * 4 + (me % 4 + 4 - dx) % 4 for dy, dx in SHIFTS]

    def node(i, _):
        n = lists[8, i]
        at = nodes[0]
        for z in range(1, 8):
            at = jnp.where(i == z, nodes[z], at)
        length = lengths[at]
        steps = (n + C - 1) // C

        def chunk(t, _, nk):
            leaves = []
            rows = []
            for c in range(C):
                leaf = lists[i, jnp.minimum(t * C + c, n - 1)]
                leaves.append(leaf)
                rows.append(q_ref[leaf // 8, pl.ds(pl.multiple_of((leaf % 8) * R, 16), R)])
            q = jnp.concatenate(rows, axis=0)
            k = kv[i, 0, :nk]
            v = kv[i, 1, :nk]
            s = lax.dot_general(q, k, (((1,), (1,)), ((), ())), preferred_element_type=jnp.float32)
            pos = iota((1, 256), 1) + (nk - 256)
            tail = jnp.where(pos < length, s[:, nk - 256:], -1e30)
            s = jnp.concatenate([s[:, :nk - 256], tail], axis=1) if nk > 256 else tail
            m = jnp.max(s, axis=1, keepdims=True)
            p = jnp.exp2((s - m) * SCALE2)
            l = jnp.sum(p, axis=1, keepdims=True)
            o = jnp.dot(p.astype(jnp.bfloat16), v, preferred_element_type=jnp.float32)
            m = jnp.broadcast_to(m * SCALE2, (C * R, 128))
            l = jnp.broadcast_to(l, (C * R, 128))
            for c in range(C):
                leaf = leaves[c]
                oc, mc, lc = (z[c * R:(c + 1) * R] for z in (o, m, l))
                live = t * C + c < n
                was = seen[leaf]

                @pl.when(live & (was == 0))
                def _():
                    acc[leaf] = oc
                    top[leaf] = mc
                    tot[leaf] = lc
                    seen[leaf] = 1

                @pl.when(live & (was == 1))
                def _():
                    m0 = top[leaf]
                    mn = jnp.maximum(m0, mc)
                    a0 = jnp.exp2(m0 - mn)
                    a1 = jnp.exp2(mc - mn)
                    top[leaf] = mn
                    tot[leaf] = tot[leaf] * a0 + lc * a1
                    acc[leaf] = acc[leaf] * a0 + oc * a1
            return 0

        quarter = (length + 255) // 256
        for b in range(1, 5):
            @pl.when(quarter == b)
            def _():
                lax.fori_loop(0, steps, functools.partial(chunk, nk=256 * b), 0)
        return 0

    lax.fori_loop(0, 8, node, 0)

    eye = iota((R, 128), 0) == iota((R, 128), 1)

    def finish(leaf, _):
        dev = leaf // 8
        slot = leaf % 8
        row = pl.multiple_of(slot * R, 16)

        @pl.when(seen[leaf] == 1)
        def _():
            w = tot[leaf]
            out_ref[dev, pl.ds(row, R)] = (acc[leaf] / w).astype(jnp.bfloat16)
            value = top[leaf] * LN2 + jnp.log(w)
            lse[dev, pl.ds(slot, 1)] = jnp.sum(jnp.where(eye, value, 0.0), axis=0, keepdims=True)

        @pl.when(seen[leaf] == 0)
        def _():
            out_ref[dev, pl.ds(row, R)] = jnp.zeros((R, 128), jnp.bfloat16)
            lse[dev, pl.ds(slot, 1)] = jnp.full((1, 128), -1e30, jnp.float32)
        return 0

    lax.fori_loop(0, 128, finish, 0)

    def split(dev, _):
        value = lse[dev]
        hi = value.astype(jnp.bfloat16).astype(jnp.float32)
        mid = (value - hi).astype(jnp.bfloat16).astype(jnp.float32)
        lo = value - hi - mid
        out_ref[dev, 640:672] = jnp.concatenate([hi, mid, lo, jnp.zeros_like(lo)], axis=0).astype(jnp.bfloat16)
        return 0

    lax.fori_loop(0, 16, split, 0)


def attend(me, lengths, q, kvs):
    smem = pl.BlockSpec(memory_space=pltpu.SMEM)
    return pl.pallas_call(
        attend_kernel,
        out_shape=jax.ShapeDtypeStruct((16, 672, 128), jnp.bfloat16),
        in_specs=[smem] * 2 + [pl.BlockSpec(memory_space=pltpu.VMEM)] + [pl.BlockSpec(memory_space=pl.ANY)] * 8,
        out_specs=pl.BlockSpec(memory_space=pltpu.VMEM),
        scratch_shapes=[
            pltpu.VMEM((8, 2, SPAN, 128), jnp.bfloat16),
            pltpu.VMEM((128, R, 128), jnp.float32),
            pltpu.VMEM((128, R, 128), jnp.float32),
            pltpu.VMEM((128, R, 128), jnp.float32),
            pltpu.VMEM((16, 8, 128), jnp.float32),
            pltpu.VMEM((16, 128), jnp.int32),
            pltpu.SMEM((16, 128), jnp.int32),
            pltpu.SMEM((128,), jnp.int32),
            pltpu.SemaphoreType.DMA((8,)),
            pltpu.SemaphoreType.DMA,
        ],
        compiler_params=pltpu.CompilerParams(vmem_limit_bytes=48 * 1024 * 1024),
        name="attend",
    )(me, lengths, q, *kvs)


def shift_pairs(dy, dx):
    return [(y * 4 + x, (y + dy) % 4 * 4 + (x + dx) % 4) for y in range(4) for x in range(4)]


def colour_of(y, x):
    return (y % 2) * 4 + (x + 2 * (y // 2)) % 4


def pack_queries_kernel(anc, q_ref, out, buf, sem):
    me = lax.axis_index("node")
    lane = iota((16, 128), 1)
    row = iota((16, 128), 0)
    named = jnp.zeros((16, 128), jnp.int32)
    for n in range(8):
        for d in range(3):
            named = jnp.where((row == d) & (lane == me * 8 + n), anc[n, d], named)
    named = named.astype(jnp.float32).astype(jnp.bfloat16)
    copies = []
    for g in range(8):
        for n in range(8):
            for j in range(5):
                at = n * R + j * 16
                head = g * 5 + j
                buf[g, at:at + 16] = q_ref[n * 16:(n + 1) * 16, head * 128:(head + 1) * 128]
        buf[g, 640:656] = named
        for t in (FIRST[g], SECOND[g]):
            copies.append(pltpu.make_async_copy(buf.at[g], out.at[t], sem.at[t]))
            copies[-1].start()
    for c in copies:
        c.wait()


def pack_queries(anc, q):
    return pl.pallas_call(
        pack_queries_kernel,
        out_shape=jax.ShapeDtypeStruct((16, 656, 128), jnp.bfloat16),
        in_specs=[pl.BlockSpec(memory_space=pltpu.SMEM), pl.BlockSpec(memory_space=pltpu.VMEM)],
        out_specs=pl.BlockSpec(memory_space=pl.ANY),
        scratch_shapes=[pltpu.VMEM((8, 656, 128), jnp.bfloat16), pltpu.SemaphoreType.DMA((16,))],
        compiler_params=pltpu.CompilerParams(vmem_limit_bytes=16 * 1024 * 1024),
        name="pack_queries",
    )(anc, q)


def pack_kv_kernel(kv_ref, *refs):
    outs, (buf, sem) = refs[:8], refs[8:]
    me = lax.axis_index("node")
    y, x = me // 4, me % 4
    loads, stores = [], []
    for i, (dy, dx) in enumerate(SHIFTS):
        at = pl.multiple_of(colour_of((y + dy) % 4, (x + dx) % 4) * 128, 128)
        for z in range(2):
            loads.append(
                pltpu.make_async_copy(kv_ref.at[z, 0, :, pl.ds(at, 128)], buf.at[i, z], sem.at[0, i, z])
            )
            stores.append(pltpu.make_async_copy(buf.at[i, z], outs[i].at[z], sem.at[1, i, z]))
    for c in loads:
        c.start()
    for c, d in zip(loads, stores):
        c.wait()
        d.start()
    for d in stores:
        d.wait()


def pack_kv(kv):
    hbm = pl.BlockSpec(memory_space=pl.ANY)
    return pl.pallas_call(
        pack_kv_kernel,
        out_shape=tuple(jax.ShapeDtypeStruct((2, SPAN, 128), jnp.bfloat16) for _ in range(8)),
        in_specs=[hbm],
        out_specs=(hbm,) * 8,
        scratch_shapes=[pltpu.VMEM((8, 2, SPAN, 128), jnp.bfloat16), pltpu.SemaphoreType.DMA((2, 8, 2))],
        compiler_params=pltpu.CompilerParams(vmem_limit_bytes=16 * 1024 * 1024),
        name="pack_kv",
    )(kv)


def self_kernel(q_ref, kv_ref, out_ref, lse_ref):
    row = lax.broadcasted_iota(jnp.int32, (640, 128), 0)
    col = lax.broadcasted_iota(jnp.int32, (640, 128), 1)
    keep = (row // R == col // 16) & (col % 16 <= row % 16)
    eye = lax.broadcasted_iota(jnp.int32, (R, 128), 0) == lax.broadcasted_iota(jnp.int32, (R, 128), 1)
    for g in range(8):
        q = jnp.concatenate(
            [
                q_ref[n * 16:(n + 1) * 16, (g * 5 + j) * 128:(g * 5 + j + 1) * 128]
                for n in range(8)
                for j in range(5)
            ],
            axis=0,
        )
        k = kv_ref[0, :, g * 128:(g + 1) * 128]
        v = kv_ref[1, :, g * 128:(g + 1) * 128]
        s = lax.dot_general(q, k, (((1,), (1,)), ((), ())), preferred_element_type=jnp.float32)
        s = jnp.where(keep, s, -1e30)
        m = jnp.max(s, axis=1, keepdims=True)
        p = jnp.exp2((s - m) * SCALE2)
        l = jnp.sum(p, axis=1, keepdims=True)
        o = jnp.dot(p.astype(jnp.bfloat16), v, preferred_element_type=jnp.float32)
        out_ref[g] = o / l
        value = jnp.broadcast_to(m * (SCALE2 * LN2) + jnp.log(l), (640, 128))
        for n in range(8):
            part = jnp.where(eye, value[n * R:(n + 1) * R], 0.0)
            lse_ref[n, g:g + 1] = jnp.sum(part, axis=0, keepdims=True)


def attend_self(q, leaf_kv):
    vmem = pl.BlockSpec(memory_space=pltpu.VMEM)
    return pl.pallas_call(
        self_kernel,
        out_shape=(
            jax.ShapeDtypeStruct((8, 640, 128), jnp.float32),
            jax.ShapeDtypeStruct((8, 8, 128), jnp.float32),
        ),
        in_specs=[vmem] * 2,
        out_specs=(vmem,) * 2,
        compiler_params=pltpu.CompilerParams(vmem_limit_bytes=32 * 1024 * 1024),
        name="attend_self",
    )(q, leaf_kv)


def merge_kernel(back_ref, codes_ref, own_ref, own_lse, out_ref, lse):
    leaf = pl.program_id(0)

    @pl.when(leaf == 0)
    def _():
        for g in range(8):
            for z, t in enumerate((FIRST[g], SECOND[g])):
                code = codes_ref[t].astype(jnp.float32)
                value = code[0:8] + code[8:16] + code[16:24]
                for n in range(8):
                    lse[z, n, g:g + 1] = value[n:n + 1]

    l0, l1, l2 = own_lse[leaf], lse[0, leaf], lse[1, leaf]
    top = jnp.maximum(l0, jnp.maximum(l1, l2))
    w0, w1, w2 = jnp.exp(l0 - top), jnp.exp(l1 - top), jnp.exp(l2 - top)
    inv = 1.0 / (w0 + w1 + w2)
    eye = lax.broadcasted_iota(jnp.int32, (R, 128), 0) == lax.broadcasted_iota(jnp.int32, (R, 128), 1)

    def spread(w, g):
        return jnp.sum(jnp.where(eye, w[g:g + 1], 0.0), axis=1, keepdims=True)

    s0, s1, s2 = w0 * inv, w1 * inv, w2 * inv
    for g in range(8):
        o = (
            spread(s0, g) * own_ref[g]
            + spread(s1, g) * back_ref[FIRST[g]].astype(jnp.float32)
            + spread(s2, g) * back_ref[SECOND[g]].astype(jnp.float32)
        )
        for j in range(5):
            out_ref[:, (g * 5 + j) * 128:(g * 5 + j + 1) * 128] = o[j * 16:(j + 1) * 16]


def merge(back, own, own_lse):
    return pl.pallas_call(
        merge_kernel,
        grid=(8,),
        out_shape=jax.ShapeDtypeStruct((128, 5120), jnp.float32),
        in_specs=[
            pl.BlockSpec((16, R, 128), lambda n: (0, n, 0)),
            pl.BlockSpec((16, 32, 128), lambda n: (0, 20, 0)),
            pl.BlockSpec((8, R, 128), lambda n: (0, n, 0)),
            pl.BlockSpec((8, 8, 128), lambda n: (0, 0, 0)),
        ],
        out_specs=pl.BlockSpec((16, 5120), lambda n: (n, 0)),
        scratch_shapes=[pltpu.VMEM((2, 8, 8, 128), jnp.float32)],
        compiler_params=pltpu.CompilerParams(vmem_limit_bytes=32 * 1024 * 1024),
        name="merge",
    )(back, back, own, own_lse)


def shards(queries, leaf_kv, node_kv, node_lengths, ancestors):
    me = lax.axis_index("node").astype(jnp.int32).reshape(1)
    outgoing = pack_queries(ancestors, queries)
    pieces = pack_kv(node_kv)
    arrived = lax.all_to_all(outgoing, "node", split_axis=0, concat_axis=0, tiled=True)
    kvs = [pieces[0]] + [
        lax.ppermute(piece, "node", shift_pairs(dy, dx)) for piece, (dy, dx) in zip(pieces[1:], SHIFTS[1:])
    ]
    own, own_lse = attend_self(queries, leaf_kv)
    answer = attend(me, node_lengths, arrived, kvs)
    back = lax.all_to_all(answer, "node", split_axis=0, concat_axis=0, tiled=True)
    return merge(back, own, own_lse)


def solution(mesh):
    placed = (
        P(("leaf", "node"), None),
        P(None, ("leaf", "node"), None),
        P(None, ("leaf", "node"), None, None),
        P("leaf"),
        P(("leaf", "node"), None),
    )
    return jax.shard_map(
        shards, mesh=mesh, in_specs=placed, out_specs=P(("leaf", "node"), None), check_vma=False
    )
```

```python
import functools
import jax
import jax.numpy as jnp
from jax import lax
from jax.experimental import pallas as pl
from jax.experimental.pallas import tpu as pltpu
from jax.sharding import PartitionSpec as P

SCALE2 = (128 ** -0.5) * 1.4426950408889634
LN2 = 0.6931471805599453
SPAN = 1024
R = 80
C = 4
SHIFTS = ((0, 0), (2, 0), (1, 1), (3, 1), (0, 1), (0, 3), (1, 0), (3, 0))
COLOUR = tuple((y % 2) * 4 + (x + 2 * (y // 2)) % 4 for y in range(4) for x in range(4))
FIRST = tuple(COLOUR.index(g) for g in range(8))
SECOND = tuple(15 - COLOUR[::-1].index(g) for g in range(8))
PARTS = 2
LV = 8 // PARTS
ROWS = LV * R
LEAVES = 16 * LV
TRASH = LEAVES
CODES = 4 * LV


def iota(shape, axis):
    return lax.broadcasted_iota(jnp.int32, shape, axis)


def rank_leaves(held, q_ref, meta, lists, sem):
    named = q_ref[0, ROWS:ROWS + 16].astype(jnp.float32)
    for src in range(1, 16):
        named = named + q_ref[src, ROWS:ROWS + 16].astype(jnp.float32)
    nodes = jnp.full((128, 128), -1, jnp.int32)
    for i, node in enumerate(held):
        nodes = jnp.where(iota((128, 128), 0) == i, node, nodes)
    nodes = nodes.astype(jnp.float32)
    member = (nodes == named[0:1]) | (nodes == named[1:2]) | (nodes == named[2:3])
    member = member & (iota((128, 128), 1) < LEAVES)
    member = jnp.where(member, 1.0, 0.0).astype(jnp.bfloat16)
    lower = jnp.where(iota((128, 128), 1) <= iota((128, 128), 0), 1.0, 0.0).astype(jnp.bfloat16)
    count = lax.dot_general(lower, member, (((1,), (1,)), ((), ())), preferred_element_type=jnp.float32)
    place = iota((128, 128), 1).astype(jnp.float32)
    for i in range(len(held)):
        before = jnp.where(count[:, i:i + 1] <= place, 1.0, 0.0)
        meta[i:i + 1] = jnp.sum(before, axis=0, keepdims=True).astype(jnp.int32)
    meta[8:9] = count[127:128].astype(jnp.int32)
    copy = pltpu.make_async_copy(meta, lists, sem)
    copy.start()
    copy.wait()


def attend_kernel(slots, first, last, me_ref, lengths, q_ref, *refs):
    held = len(slots)
    kv_in, refs = refs[:held], refs[held:]
    if not first:
        state_in, refs = refs[:2], refs[2:]
    if last:
        out_ref, refs = refs[0], refs[1:]
    else:
        state_out, refs = refs[:2], refs[2:]
    (kv, acc, top, tot, sa, sb, meta, lists, seen, items, lens, sem, meta_sem, state_sem, *refs) = refs
    copies = []
    for i in range(held):
        for z in range(2):
            copies.append(
                pltpu.make_async_copy(kv_in[i].at[z], kv.at[i, z], sem.at[i, z])
            )
    if not first:
        for z, (a, b) in enumerate(zip(state_in, (acc, top))):
            copies.append(pltpu.make_async_copy(a, b.at[0:LEAVES], state_sem.at[z]))
    for c in copies:
        c.start()
    me = me_ref[0]
    nodes = [(me // 4 + 4 - dy) % 4 * 4 + (me % 4 + 4 - dx) % 4 for dy, dx in (SHIFTS[i] for i in slots)]
    for i in range(held):
        lens[i] = lengths[nodes[i]]

    def clear(i, _):
        seen[i] = 0
        return 0

    lax.fori_loop(0, LEAVES + 1, clear, 0)
    rank_leaves(nodes, q_ref, meta, lists, meta_sem)

    bounds = []
    cursor = jnp.int32(0)
    for b in range(1, 5):
        start = cursor

        def node(i, cur):
            n = jnp.where((lens[i] + 255) // 256 == b, lists[8, i], 0)

            def some(k, cur):
                items[0, cur] = i
                for z in range(C):
                    leaf = lists[i, jnp.minimum(C * k + z, n - 1)]
                    dest = jnp.where(C * k + z < n, leaf, TRASH)
                    items[1 + z, cur] = leaf + dest * 256 + seen[dest] * 65536
                    seen[dest] = 1
                return cur + 1

            return lax.fori_loop(0, (n + C - 1) // C, some, cur)

        cursor = lax.fori_loop(0, held, node, start)
        odd = (cursor - start) % 2

        @pl.when(odd == 1)
        def _():
            items[0, cursor] = items[0, cursor - 1]
            for z in range(C):
                items[1 + z, cursor] = items[1 + z, cursor - 1] % 256 + TRASH * 256

        cursor = cursor + odd
        bounds.append((start, cursor))

    for c in copies:
        c.wait()

    def scores(t, nk):
        leaves = [items[1 + z, t] % 256 for z in range(C)]
        q = jnp.concatenate(
            [q_ref[n // LV, pl.ds(pl.multiple_of(n % LV * R, 16), R)] for n in leaves], axis=0
        )
        return lax.dot_general(
            q, kv[items[0, t], 0, :nk], (((1,), (1,)), ((), ())), preferred_element_type=jnp.float32
        )

    def soften(s_ref, t, nk):
        i = items[0, t]
        keep = iota((1, 256), 1) + (nk - 256) < lens[i]
        s = jnp.where(keep, s_ref[:, nk - 256:nk], -1e30)
        if nk > 256:
            s = jnp.concatenate([s_ref[:, :nk - 256], s], axis=1)
        m = jnp.max(s, axis=1, keepdims=True)
        p = jnp.exp2((s - m) * SCALE2).astype(jnp.bfloat16)
        v = jnp.concatenate([kv[i, 1, :nk], jnp.ones((nk, 128), jnp.bfloat16)], axis=1)
        o = jnp.dot(p, v, preferred_element_type=jnp.float32)
        m = jnp.broadcast_to(m * SCALE2, (C * R, 128))
        for z in range(C):
            code = items[1 + z, t]
            at = code // 256 % 256
            old = code >= 65536
            mz = m[z * R:(z + 1) * R]
            oz = o[z * R:(z + 1) * R]
            if first:
                m0 = jnp.where(old, top[at], -1e30)
                w0 = jnp.where(old, tot[at], 0.0)
                a0 = jnp.where(old, acc[at], 0.0)
            else:
                m0 = top[at]
                w0 = jnp.where(old, tot[at], 1.0)
                a0 = acc[at]
            mn = jnp.maximum(m0, mz)
            e0 = jnp.exp2(m0 - mn)
            e1 = jnp.exp2(mz - mn)
            top[at] = mn
            tot[at] = w0 * e0 + oz[:, 128:256] * e1
            acc[at] = a0 * e0 + oz[:, 0:128] * e1

    for b, (start, end) in enumerate(bounds):
        nk = 256 * (b + 1)

        @pl.when(end > start)
        def _():
            sa[:, :nk] = scores(start, nk)

            def step(u, _):
                t = start + 2 * u
                sb[:, :nk] = scores(t + 1, nk)
                soften(sa, t, nk)
                sa[:, :nk] = scores(jnp.minimum(t + 2, end - 1), nk)
                soften(sb, t + 1, nk)
                return 0

            lax.fori_loop(0, (end - start) // 2, step, 0)

    def load(n):
        old = seen[n] == 1
        if first:
            return (
                jnp.where(old, acc[n], 0.0),
                jnp.where(old, top[n], -1e30),
                jnp.where(old, tot[n], 1.0),
            )
        return acc[n], top[n], jnp.where(old, tot[n], 1.0)

    if not last:

        def even(i, _):
            for z in range(4):
                n = i * 4 + z
                a, m, w = load(n)
                acc[n] = a / w
                top[n] = m + jnp.log2(w)
            return 0

        lax.fori_loop(0, LEAVES // 4, even, 0)
        copies = [
            pltpu.make_async_copy(a.at[0:LEAVES], b, state_sem.at[z])
            for z, (a, b) in enumerate(zip((acc, top), state_out))
        ]
        for c in copies:
            c.start()
        for c in copies:
            c.wait()
        return

    out_buf, out_sem = refs
    eye = iota((R, 128), 0) == iota((R, 128), 1)

    def pick(x):
        return jnp.sum(jnp.where(eye, x, 0.0), axis=0, keepdims=True)

    def finish(dev, _):
        tops, tots = [], []
        for n in range(LV):
            a, m, w = load(dev * LV + n)
            out_buf[dev, n * R:(n + 1) * R] = (a / w).astype(jnp.bfloat16)
            tops.append(pick(m))
            tots.append(pick(w))
        used = iota((LV, 128), 1) < R
        tots = jnp.where(used, jnp.concatenate(tots, axis=0), 1.0)
        value = jnp.concatenate(tops, axis=0) * LN2 + jnp.log(tots)
        hi = value.astype(jnp.bfloat16).astype(jnp.float32)
        mid = (value - hi).astype(jnp.bfloat16).astype(jnp.float32)
        lo = value - hi - mid
        codes = jnp.concatenate([hi, mid, lo, jnp.zeros_like(lo)], axis=0)
        out_buf[dev, ROWS:ROWS + CODES] = codes.astype(jnp.bfloat16)
        pltpu.make_async_copy(out_buf.at[dev], out_ref.at[dev], out_sem.at[dev]).start()
        return 0

    lax.fori_loop(0, 16, finish, 0)
    for dev in range(16):
        pltpu.make_async_copy(out_buf.at[dev], out_ref.at[dev], out_sem.at[dev]).wait()


def attend(me, lengths, q, kvs, slots=tuple(range(8)), state=None, last=True):
    smem = pl.BlockSpec(memory_space=pltpu.SMEM)
    vmem = pl.BlockSpec(memory_space=pltpu.VMEM)
    hbm = pl.BlockSpec(memory_space=pl.ANY)
    f32 = jnp.float32
    first = state is None
    held = len(slots)
    if last:
        out_shape, out_specs = jax.ShapeDtypeStruct((16, ROWS + CODES, 128), jnp.bfloat16), hbm
    else:
        out_shape, out_specs = (jax.ShapeDtypeStruct((LEAVES, R, 128), f32),) * 2, (hbm,) * 2
    extra = () if first else state
    scratch = [
        pltpu.VMEM((held, 2, SPAN, 128), jnp.bfloat16),
        pltpu.VMEM((LEAVES + 1, R, 128), f32),
        pltpu.VMEM((LEAVES + 1, R, 128), f32),
        pltpu.VMEM((LEAVES + 1, R, 128), f32),
        pltpu.VMEM((C * R, SPAN), f32),
        pltpu.VMEM((C * R, SPAN), f32),
        pltpu.VMEM((16, 128), jnp.int32),
        pltpu.SMEM((16, 128), jnp.int32),
        pltpu.SMEM((LEAVES + 1,), jnp.int32),
        pltpu.SMEM((1 + C, 128), jnp.int32),
        pltpu.SMEM((8,), jnp.int32),
        pltpu.SemaphoreType.DMA((held, 2)),
        pltpu.SemaphoreType.DMA,
        pltpu.SemaphoreType.DMA((2,)),
    ]
    if last:
        scratch += [pltpu.VMEM((16, ROWS + CODES, 128), jnp.bfloat16), pltpu.SemaphoreType.DMA((16,))]
    return pl.pallas_call(
        functools.partial(attend_kernel, slots, first, last),
        out_shape=out_shape,
        in_specs=[smem] * 2 + [vmem] + [hbm] * (held + len(extra)),
        out_specs=out_specs,
        scratch_shapes=scratch,
        compiler_params=pltpu.CompilerParams(vmem_limit_bytes=56 * 1024 * 1024),
        name="attend" if last else "attend_near",
    )(me, lengths, q, *kvs, *extra)


def shift_pairs(dy, dx):
    return [(y * 4 + x, (y + dy) % 4 * 4 + (x + dx) % 4) for y in range(4) for x in range(4)]


def colour_of(y, x):
    return (y % 2) * 4 + (x + 2 * (y // 2)) % 4


def pack_queries_kernel(anc, q_ref, *refs):
    outs, (buf, sem) = refs[:PARTS], refs[PARTS:]
    me = lax.axis_index("node")
    lane = iota((16, 128), 1)
    row = iota((16, 128), 0)
    copies = []
    for part in range(PARTS):
        named = jnp.zeros((16, 128), jnp.int32)
        for n in range(LV):
            for d in range(3):
                named = jnp.where((row == d) & (lane == me * LV + n), anc[part * LV + n, d], named)
        named = named.astype(jnp.float32).astype(jnp.bfloat16)
        for g in range(8):
            for n in range(LV):
                for j in range(5):
                    at = n * R + j * 16
                    head = g * 5 + j
                    tok = (part * LV + n) * 16
                    buf[part, g, at:at + 16] = q_ref[tok:tok + 16, head * 128:(head + 1) * 128]
            buf[part, g, ROWS:ROWS + 16] = named
            for t in (FIRST[g], SECOND[g]):
                copies.append(pltpu.make_async_copy(buf.at[part, g], outs[part].at[t], sem.at[part, t]))
                copies[-1].start()
    for c in copies:
        c.wait()


def pack_queries(anc, q):
    hbm = pl.BlockSpec(memory_space=pl.ANY)
    return pl.pallas_call(
        pack_queries_kernel,
        out_shape=(jax.ShapeDtypeStruct((16, ROWS + 16, 128), jnp.bfloat16),) * PARTS,
        in_specs=[pl.BlockSpec(memory_space=pltpu.SMEM), pl.BlockSpec(memory_space=pltpu.VMEM)],
        out_specs=(hbm,) * PARTS,
        scratch_shapes=[
            pltpu.VMEM((PARTS, 8, ROWS + 16, 128), jnp.bfloat16),
            pltpu.SemaphoreType.DMA((PARTS, 16)),
        ],
        compiler_params=pltpu.CompilerParams(vmem_limit_bytes=16 * 1024 * 1024),
        name="pack_queries",
    )(anc, q)


def pack_kv_kernel(kv_ref, *refs):
    outs, (buf, sem) = refs[:8], refs[8:]
    me = lax.axis_index("node")
    y, x = me // 4, me % 4
    loads, stores = [], []
    for i, (dy, dx) in enumerate(SHIFTS):
        at = pl.multiple_of(colour_of((y + dy) % 4, (x + dx) % 4) * 128, 128)
        for z in range(2):
            loads.append(
                pltpu.make_async_copy(kv_ref.at[z, 0, :, pl.ds(at, 128)], buf.at[i, z], sem.at[0, i, z])
            )
            stores.append(pltpu.make_async_copy(buf.at[i, z], outs[i].at[z], sem.at[1, i, z]))
    for c in loads:
        c.start()
    for c, d in zip(loads, stores):
        c.wait()
        d.start()
    for d in stores:
        d.wait()


def pack_kv(kv):
    hbm = pl.BlockSpec(memory_space=pl.ANY)
    return pl.pallas_call(
        pack_kv_kernel,
        out_shape=tuple(jax.ShapeDtypeStruct((2, SPAN, 128), jnp.bfloat16) for _ in range(8)),
        in_specs=[hbm],
        out_specs=(hbm,) * 8,
        scratch_shapes=[pltpu.VMEM((8, 2, SPAN, 128), jnp.bfloat16), pltpu.SemaphoreType.DMA((2, 8, 2))],
        compiler_params=pltpu.CompilerParams(vmem_limit_bytes=16 * 1024 * 1024),
        name="pack_kv",
    )(kv)


def self_kernel(q_ref, kv_ref, out_ref, lse_ref):
    row = lax.broadcasted_iota(jnp.int32, (640, 128), 0)
    col = lax.broadcasted_iota(jnp.int32, (640, 128), 1)
    keep = (row // R == col // 16) & (col % 16 <= row % 16)
    eye = lax.broadcasted_iota(jnp.int32, (R, 128), 0) == lax.broadcasted_iota(jnp.int32, (R, 128), 1)
    for g in range(8):
        q = jnp.concatenate(
            [
                q_ref[n * 16:(n + 1) * 16, (g * 5 + j) * 128:(g * 5 + j + 1) * 128]
                for n in range(8)
                for j in range(5)
            ],
            axis=0,
        )
        k = kv_ref[0, :, g * 128:(g + 1) * 128]
        v = kv_ref[1, :, g * 128:(g + 1) * 128]
        s = lax.dot_general(q, k, (((1,), (1,)), ((), ())), preferred_element_type=jnp.float32)
        s = jnp.where(keep, s, -1e30)
        m = jnp.max(s, axis=1, keepdims=True)
        p = jnp.exp2((s - m) * SCALE2)
        l = jnp.sum(p, axis=1, keepdims=True)
        o = jnp.dot(p.astype(jnp.bfloat16), v, preferred_element_type=jnp.float32)
        out_ref[g] = o / l
        value = jnp.broadcast_to(m * (SCALE2 * LN2) + jnp.log(l), (640, 128))
        for n in range(8):
            part = jnp.where(eye, value[n * R:(n + 1) * R], 0.0)
            lse_ref[n, g:g + 1] = jnp.sum(part, axis=0, keepdims=True)


def attend_self(q, leaf_kv):
    vmem = pl.BlockSpec(memory_space=pltpu.VMEM)
    return pl.pallas_call(
        self_kernel,
        out_shape=(
            jax.ShapeDtypeStruct((8, 640, 128), jnp.float32),
            jax.ShapeDtypeStruct((8, 8, 128), jnp.float32),
        ),
        in_specs=[vmem] * 2,
        out_specs=(vmem,) * 2,
        compiler_params=pltpu.CompilerParams(vmem_limit_bytes=32 * 1024 * 1024),
        name="attend_self",
    )(q, leaf_kv)


def merge_kernel(part, back_ref, codes_ref, own_ref, own_lse, *refs):
    out_ref, lse = refs[-2:]
    leaf = pl.program_id(0)

    @pl.when(leaf == 0)
    def _():
        for g in range(8):
            for z, t in enumerate((FIRST[g], SECOND[g])):
                code = codes_ref[t].astype(jnp.float32)
                value = code[0:LV] + code[LV:2 * LV] + code[2 * LV:3 * LV]
                for n in range(LV):
                    lse[z, n, g:g + 1] = value[n:n + 1]

    l0, l1, l2 = own_lse[leaf + part * LV], lse[0, leaf], lse[1, leaf]
    top = jnp.maximum(l0, jnp.maximum(l1, l2))
    w0, w1, w2 = jnp.exp(l0 - top), jnp.exp(l1 - top), jnp.exp(l2 - top)
    inv = 1.0 / (w0 + w1 + w2)
    eye = iota((R, 128), 0) == iota((R, 128), 1)

    def spread(w, g):
        return jnp.sum(jnp.where(eye, w[g:g + 1], 0.0), axis=1, keepdims=True)

    s0, s1, s2 = w0 * inv, w1 * inv, w2 * inv
    for g in range(8):
        o = (
            spread(s0, g) * own_ref[g]
            + spread(s1, g) * back_ref[FIRST[g]].astype(jnp.float32)
            + spread(s2, g) * back_ref[SECOND[g]].astype(jnp.float32)
        )
        for j in range(5):
            out_ref[:, (g * 5 + j) * 128:(g * 5 + j + 1) * 128] = o[j * 16:(j + 1) * 16]


def merge(part, back, own, own_lse, before):
    in_specs = [
        pl.BlockSpec((16, R, 128), lambda n: (0, n, 0)),
        pl.BlockSpec((16, CODES, 128), lambda n: (0, ROWS // CODES, 0)),
        pl.BlockSpec((8, R, 128), lambda n: (0, n + part * LV, 0)),
        pl.BlockSpec((8, 8, 128), lambda n: (0, 0, 0)),
    ]
    args = [back, back, own, own_lse]
    if before is not None:
        in_specs.append(pl.BlockSpec(memory_space=pl.ANY))
        args.append(before)
    return pl.pallas_call(
        functools.partial(merge_kernel, part),
        grid=(LV,),
        out_shape=jax.ShapeDtypeStruct((128, 5120), jnp.float32),
        in_specs=in_specs,
        out_specs=pl.BlockSpec((16, 5120), lambda n: (n + part * LV, 0)),
        scratch_shapes=[pltpu.VMEM((2, 8, 8, 128), jnp.float32)],
        input_output_aliases={} if before is None else {4: 0},
        compiler_params=pltpu.CompilerParams(vmem_limit_bytes=32 * 1024 * 1024),
        name="merge",
    )(*args)


def shards(queries, leaf_kv, node_kv, node_lengths, ancestors):
    me = lax.axis_index("node").astype(jnp.int32).reshape(1)
    outgoing = list(pack_queries(ancestors, queries))
    pieces = pack_kv(node_kv)
    kvs = [pieces[0]] + [
        lax.ppermute(piece, "node", shift_pairs(dy, dx)) for piece, (dy, dx) in zip(pieces[1:], SHIFTS[1:])
    ]

    def swap(x):
        return lax.all_to_all(x, "node", split_axis=0, concat_axis=0, tiled=True)

    arrived = [swap(outgoing[0])]
    outgoing[1], *kvs = lax.optimization_barrier((outgoing[1], *kvs))
    arrived.append(swap(outgoing[1]))
    own, own_lse = attend_self(queries, leaf_kv)
    out = None
    for part in range(PARTS):
        answer = attend(me, node_lengths, arrived[part], kvs)
        out = merge(part, swap(answer), own, own_lse, out)
    return out


def solution(mesh):
    placed = (
        P(("leaf", "node"), None),
        P(None, ("leaf", "node"), None),
        P(None, ("leaf", "node"), None, None),
        P("leaf"),
        P(("leaf", "node"), None),
    )
    return jax.shard_map(
        shards, mesh=mesh, in_specs=placed, out_specs=P(("leaf", "node"), None), check_vma=False
    )
```

```python
import functools
import jax
import jax.numpy as jnp
from jax import lax
from jax.experimental import pallas as pl
from jax.experimental.pallas import tpu as pltpu
from jax.sharding import PartitionSpec as P

SCALE2 = (128 ** -0.5) * 1.4426950408889634
LN2 = 0.6931471805599453
SPAN = 1024
R = 80
C = 4
SHIFTS = (
    ((0, 0), (0, 0)),
    ((2, 0), (0, 2)),
    ((1, 1), (3, 3)),
    ((3, 1), (1, 3)),
    ((0, 1), (0, 1)),
    ((0, 3), (0, 3)),
    ((1, 0), (1, 0)),
    ((3, 0), (3, 0)),
)
COLOUR = tuple((y % 2) * 4 + (x + 2 * (y // 2)) % 4 for y in range(4) for x in range(4))
FIRST = tuple(COLOUR.index(g) for g in range(8))
SECOND = tuple(15 - COLOUR[::-1].index(g) for g in range(8))
PARTS = 2
LV = 8 // PARTS
ROWS = LV * R
LEAVES = 16 * LV
TRASH = LEAVES
CODES = 4 * LV


def iota(shape, axis):
    return lax.broadcasted_iota(jnp.int32, shape, axis)


def rank_leaves(held, q_ref, meta, lists, sem):
    named = q_ref[0, ROWS:ROWS + 16].astype(jnp.float32)
    for src in range(1, 16):
        named = named + q_ref[src, ROWS:ROWS + 16].astype(jnp.float32)
    nodes = jnp.full((128, 128), -1, jnp.int32)
    for i, node in enumerate(held):
        nodes = jnp.where(iota((128, 128), 0) == i, node, nodes)
    nodes = nodes.astype(jnp.float32)
    member = (nodes == named[0:1]) | (nodes == named[1:2]) | (nodes == named[2:3])
    member = member & (iota((128, 128), 1) < LEAVES)
    member = jnp.where(member, 1.0, 0.0).astype(jnp.bfloat16)
    lower = jnp.where(iota((128, 128), 1) <= iota((128, 128), 0), 1.0, 0.0).astype(jnp.bfloat16)
    count = lax.dot_general(lower, member, (((1,), (1,)), ((), ())), preferred_element_type=jnp.float32)
    place = iota((128, 128), 1).astype(jnp.float32)
    for i in range(len(held)):
        before = jnp.where(count[:, i:i + 1] <= place, 1.0, 0.0)
        meta[i:i + 1] = jnp.sum(before, axis=0, keepdims=True).astype(jnp.int32)
    meta[8:9] = count[127:128].astype(jnp.int32)
    copy = pltpu.make_async_copy(meta, lists, sem)
    copy.start()
    copy.wait()


def attend_kernel(slots, first, last, me_ref, lengths, q_ref, *refs):
    held = len(slots)
    kv_in, refs = refs[:held], refs[held:]
    if not first:
        state_in, refs = refs[:2], refs[2:]
    if last:
        out_ref, refs = refs[0], refs[1:]
    else:
        state_out, refs = refs[:2], refs[2:]
    (kv, acc, top, tot, sa, sb, meta, lists, seen, items, lens, sem, meta_sem, state_sem, *refs) = refs
    copies = []
    for i in range(held):
        for z in range(2):
            copies.append(
                pltpu.make_async_copy(kv_in[i].at[z], kv.at[i, z], sem.at[i, z])
            )
    if not first:
        for z, (a, b) in enumerate(zip(state_in, (acc, top))):
            copies.append(pltpu.make_async_copy(a, b.at[0:LEAVES], state_sem.at[z]))
    for c in copies:
        c.start()
    me = me_ref[0]
    core = me_ref[1]
    nodes = []
    for i in slots:
        dy, dx = (jnp.where(core == 0, a, b) for a, b in zip(*SHIFTS[i]))
        nodes.append((me // 4 + 4 - dy) % 4 * 4 + (me % 4 + 4 - dx) % 4)
    for i in range(held):
        lens[i] = lengths[nodes[i]]

    def clear(i, _):
        seen[i] = 0
        return 0

    lax.fori_loop(0, LEAVES + 1, clear, 0)
    rank_leaves(nodes, q_ref, meta, lists, meta_sem)

    bounds = []
    cursor = jnp.int32(0)
    for b in range(1, 5):
        start = cursor

        def node(i, cur):
            n = jnp.where((lens[i] + 255) // 256 == b, lists[8, i], 0)

            def some(k, cur):
                items[0, cur] = i
                for z in range(C):
                    leaf = lists[i, jnp.minimum(C * k + z, n - 1)]
                    dest = jnp.where(C * k + z < n, leaf, TRASH)
                    items[1 + z, cur] = leaf + dest * 256 + seen[dest] * 65536
                    seen[dest] = 1
                return cur + 1

            return lax.fori_loop(0, (n + C - 1) // C, some, cur)

        cursor = lax.fori_loop(0, held, node, start)
        odd = (cursor - start) % 2

        @pl.when(odd == 1)
        def _():
            items[0, cursor] = items[0, cursor - 1]
            for z in range(C):
                items[1 + z, cursor] = items[1 + z, cursor - 1] % 256 + TRASH * 256

        cursor = cursor + odd
        bounds.append((start, cursor))

    for c in copies:
        c.wait()

    def scores(t, nk):
        leaves = [items[1 + z, t] % 256 for z in range(C)]
        q = jnp.concatenate(
            [q_ref[n // LV, pl.ds(pl.multiple_of(n % LV * R, 16), R)] for n in leaves], axis=0
        )
        return lax.dot_general(
            q, kv[items[0, t], 0, :nk], (((1,), (1,)), ((), ())), preferred_element_type=jnp.float32
        )

    def soften(s_ref, t, nk):
        i = items[0, t]
        keep = iota((1, 256), 1) + (nk - 256) < lens[i]
        s = jnp.where(keep, s_ref[:, nk - 256:nk], -1e30)
        if nk > 256:
            s = jnp.concatenate([s_ref[:, :nk - 256], s], axis=1)
        m = jnp.max(s, axis=1, keepdims=True)
        p = jnp.exp2((s - m) * SCALE2).astype(jnp.bfloat16)
        v = jnp.concatenate([kv[i, 1, :nk], jnp.ones((nk, 128), jnp.bfloat16)], axis=1)
        o = jnp.dot(p, v, preferred_element_type=jnp.float32)
        m = jnp.broadcast_to(m * SCALE2, (C * R, 128))
        for z in range(C):
            code = items[1 + z, t]
            at = code // 256 % 256
            old = code >= 65536
            mz = m[z * R:(z + 1) * R]
            oz = o[z * R:(z + 1) * R]
            if first:
                m0 = jnp.where(old, top[at], -1e30)
                w0 = jnp.where(old, tot[at], 0.0)
                a0 = jnp.where(old, acc[at], 0.0)
            else:
                m0 = top[at]
                w0 = jnp.where(old, tot[at], 1.0)
                a0 = acc[at]
            mn = jnp.maximum(m0, mz)
            e0 = jnp.exp2(m0 - mn)
            e1 = jnp.exp2(mz - mn)
            top[at] = mn
            tot[at] = w0 * e0 + oz[:, 128:256] * e1
            acc[at] = a0 * e0 + oz[:, 0:128] * e1

    for b, (start, end) in enumerate(bounds):
        nk = 256 * (b + 1)

        @pl.when(end > start)
        def _():
            sa[:, :nk] = scores(start, nk)

            def step(u, _):
                t = start + 2 * u
                sb[:, :nk] = scores(t + 1, nk)
                soften(sa, t, nk)
                sa[:, :nk] = scores(jnp.minimum(t + 2, end - 1), nk)
                soften(sb, t + 1, nk)
                return 0

            lax.fori_loop(0, (end - start) // 2, step, 0)

    def load(n):
        old = seen[n] == 1
        if first:
            return (
                jnp.where(old, acc[n], 0.0),
                jnp.where(old, top[n], -1e30),
                jnp.where(old, tot[n], 1.0),
            )
        return acc[n], top[n], jnp.where(old, tot[n], 1.0)

    if not last:

        def even(i, _):
            for z in range(4):
                n = i * 4 + z
                a, m, w = load(n)
                acc[n] = a / w
                top[n] = m + jnp.log2(w)
            return 0

        lax.fori_loop(0, LEAVES // 4, even, 0)
        copies = [
            pltpu.make_async_copy(a.at[0:LEAVES], b, state_sem.at[z])
            for z, (a, b) in enumerate(zip((acc, top), state_out))
        ]
        for c in copies:
            c.start()
        for c in copies:
            c.wait()
        return

    out_buf, out_sem = refs
    eye = iota((R, 128), 0) == iota((R, 128), 1)

    def pick(x):
        return jnp.sum(jnp.where(eye, x, 0.0), axis=0, keepdims=True)

    def finish(dev, _):
        tops, tots = [], []
        for n in range(LV):
            a, m, w = load(dev * LV + n)
            out_buf[dev, n * R:(n + 1) * R] = (a / w).astype(jnp.bfloat16)
            tops.append(pick(m))
            tots.append(pick(w))
        used = iota((LV, 128), 1) < R
        tots = jnp.where(used, jnp.concatenate(tots, axis=0), 1.0)
        value = jnp.concatenate(tops, axis=0) * LN2 + jnp.log(tots)
        hi = value.astype(jnp.bfloat16).astype(jnp.float32)
        mid = (value - hi).astype(jnp.bfloat16).astype(jnp.float32)
        lo = value - hi - mid
        codes = jnp.concatenate([hi, mid, lo, jnp.zeros_like(lo)], axis=0)
        out_buf[dev, ROWS:ROWS + CODES] = codes.astype(jnp.bfloat16)
        pltpu.make_async_copy(out_buf.at[dev], out_ref.at[dev], out_sem.at[dev]).start()
        return 0

    lax.fori_loop(0, 16, finish, 0)
    for dev in range(16):
        pltpu.make_async_copy(out_buf.at[dev], out_ref.at[dev], out_sem.at[dev]).wait()


def attend(me, lengths, q, kvs, slots=tuple(range(8)), state=None, last=True):
    smem = pl.BlockSpec(memory_space=pltpu.SMEM)
    vmem = pl.BlockSpec(memory_space=pltpu.VMEM)
    hbm = pl.BlockSpec(memory_space=pl.ANY)
    f32 = jnp.float32
    first = state is None
    held = len(slots)
    if last:
        out_shape, out_specs = jax.ShapeDtypeStruct((16, ROWS + CODES, 128), jnp.bfloat16), hbm
    else:
        out_shape, out_specs = (jax.ShapeDtypeStruct((LEAVES, R, 128), f32),) * 2, (hbm,) * 2
    extra = () if first else state
    scratch = [
        pltpu.VMEM((held, 2, SPAN, 128), jnp.bfloat16),
        pltpu.VMEM((LEAVES + 1, R, 128), f32),
        pltpu.VMEM((LEAVES + 1, R, 128), f32),
        pltpu.VMEM((LEAVES + 1, R, 128), f32),
        pltpu.VMEM((C * R, SPAN), f32),
        pltpu.VMEM((C * R, SPAN), f32),
        pltpu.VMEM((16, 128), jnp.int32),
        pltpu.SMEM((16, 128), jnp.int32),
        pltpu.SMEM((LEAVES + 1,), jnp.int32),
        pltpu.SMEM((1 + C, 128), jnp.int32),
        pltpu.SMEM((8,), jnp.int32),
        pltpu.SemaphoreType.DMA((held, 2)),
        pltpu.SemaphoreType.DMA,
        pltpu.SemaphoreType.DMA((2,)),
    ]
    if last:
        scratch += [pltpu.VMEM((16, ROWS + CODES, 128), jnp.bfloat16), pltpu.SemaphoreType.DMA((16,))]
    return pl.pallas_call(
        functools.partial(attend_kernel, slots, first, last),
        out_shape=out_shape,
        in_specs=[smem] * 2 + [vmem] + [hbm] * (held + len(extra)),
        out_specs=out_specs,
        scratch_shapes=scratch,
        compiler_params=pltpu.CompilerParams(vmem_limit_bytes=56 * 1024 * 1024),
        cost_estimate=pl.CostEstimate(
            flops=held * 2_000_000_000, bytes_accessed=held * 2_000_000, transcendentals=held * 1_000_000
        ),
        name="attend" if last else "attend_near",
    )(me, lengths, q, *kvs, *extra)


def travel_pairs(i):
    pairs = []
    for tree in range(8):
        dy, dx = SHIFTS[i][tree % 2]
        for y in range(4):
            for x in range(4):
                pairs.append((tree * 16 + y * 4 + x, tree * 16 + (y + dy) % 4 * 4 + (x + dx) % 4))
    return pairs


def colour_of(y, x):
    return (y % 2) * 4 + (x + 2 * (y // 2)) % 4


def pack_queries_kernel(anc, q_ref, *refs):
    outs, (buf, sem) = refs[:PARTS], refs[PARTS:]
    me = lax.axis_index("node")
    lane = iota((16, 128), 1)
    row = iota((16, 128), 0)
    copies = []
    for part in range(PARTS):
        named = jnp.zeros((16, 128), jnp.int32)
        for n in range(LV):
            for d in range(3):
                named = jnp.where((row == d) & (lane == me * LV + n), anc[part * LV + n, d], named)
        named = named.astype(jnp.float32).astype(jnp.bfloat16)
        for g in range(8):
            for n in range(LV):
                for j in range(5):
                    at = n * R + j * 16
                    head = g * 5 + j
                    tok = (part * LV + n) * 16
                    buf[part, g, at:at + 16] = q_ref[tok:tok + 16, head * 128:(head + 1) * 128]
            buf[part, g, ROWS:ROWS + 16] = named
            for t in (FIRST[g], SECOND[g]):
                copies.append(pltpu.make_async_copy(buf.at[part, g], outs[part].at[t], sem.at[part, t]))
                copies[-1].start()
    for c in copies:
        c.wait()


def pack_queries(anc, q):
    hbm = pl.BlockSpec(memory_space=pl.ANY)
    return pl.pallas_call(
        pack_queries_kernel,
        out_shape=(jax.ShapeDtypeStruct((16, ROWS + 16, 128), jnp.bfloat16),) * PARTS,
        in_specs=[pl.BlockSpec(memory_space=pltpu.SMEM), pl.BlockSpec(memory_space=pltpu.VMEM)],
        out_specs=(hbm,) * PARTS,
        scratch_shapes=[
            pltpu.VMEM((PARTS, 8, ROWS + 16, 128), jnp.bfloat16),
            pltpu.SemaphoreType.DMA((PARTS, 16)),
        ],
        compiler_params=pltpu.CompilerParams(vmem_limit_bytes=16 * 1024 * 1024),
        name="pack_queries",
    )(anc, q)


def pack_kv_kernel(kv_ref, *refs):
    outs, (buf, sem) = refs[:8], refs[8:]
    me = lax.axis_index("node")
    y, x = me // 4, me % 4
    loads, stores = [], []
    core = lax.axis_index("leaf") % 2
    for i in range(8):
        dy, dx = (jnp.where(core == 0, a, b) for a, b in zip(*SHIFTS[i]))
        at = pl.multiple_of(colour_of((y + dy) % 4, (x + dx) % 4) * 128, 128)
        for z in range(2):
            loads.append(
                pltpu.make_async_copy(kv_ref.at[z, 0, :, pl.ds(at, 128)], buf.at[i, z], sem.at[0, i, z])
            )
            stores.append(pltpu.make_async_copy(buf.at[i, z], outs[i].at[z], sem.at[1, i, z]))
    for c in loads:
        c.start()
    for c, d in zip(loads, stores):
        c.wait()
        d.start()
    for d in stores:
        d.wait()


def pack_kv(kv):
    hbm = pl.BlockSpec(memory_space=pl.ANY)
    return pl.pallas_call(
        pack_kv_kernel,
        out_shape=tuple(jax.ShapeDtypeStruct((2, SPAN, 128), jnp.bfloat16) for _ in range(8)),
        in_specs=[hbm],
        out_specs=(hbm,) * 8,
        scratch_shapes=[pltpu.VMEM((8, 2, SPAN, 128), jnp.bfloat16), pltpu.SemaphoreType.DMA((2, 8, 2))],
        compiler_params=pltpu.CompilerParams(vmem_limit_bytes=16 * 1024 * 1024),
        name="pack_kv",
    )(kv)


def self_kernel(q_ref, kv_ref, out_ref, lse_ref):
    row = lax.broadcasted_iota(jnp.int32, (640, 128), 0)
    col = lax.broadcasted_iota(jnp.int32, (640, 128), 1)
    keep = (row // R == col // 16) & (col % 16 <= row % 16)
    eye = lax.broadcasted_iota(jnp.int32, (R, 128), 0) == lax.broadcasted_iota(jnp.int32, (R, 128), 1)
    for g in range(8):
        q = jnp.concatenate(
            [
                q_ref[n * 16:(n + 1) * 16, (g * 5 + j) * 128:(g * 5 + j + 1) * 128]
                for n in range(8)
                for j in range(5)
            ],
            axis=0,
        )
        k = kv_ref[0, :, g * 128:(g + 1) * 128]
        v = kv_ref[1, :, g * 128:(g + 1) * 128]
        s = lax.dot_general(q, k, (((1,), (1,)), ((), ())), preferred_element_type=jnp.float32)
        s = jnp.where(keep, s, -1e30)
        m = jnp.max(s, axis=1, keepdims=True)
        p = jnp.exp2((s - m) * SCALE2)
        l = jnp.sum(p, axis=1, keepdims=True)
        o = jnp.dot(p.astype(jnp.bfloat16), v, preferred_element_type=jnp.float32)
        out_ref[g] = o / l
        value = jnp.broadcast_to(m * (SCALE2 * LN2) + jnp.log(l), (640, 128))
        for n in range(8):
            part = jnp.where(eye, value[n * R:(n + 1) * R], 0.0)
            lse_ref[n, g:g + 1] = jnp.sum(part, axis=0, keepdims=True)


def attend_self(q, leaf_kv):
    vmem = pl.BlockSpec(memory_space=pltpu.VMEM)
    return pl.pallas_call(
        self_kernel,
        out_shape=(
            jax.ShapeDtypeStruct((8, 640, 128), jnp.float32),
            jax.ShapeDtypeStruct((8, 8, 128), jnp.float32),
        ),
        in_specs=[vmem] * 2,
        out_specs=(vmem,) * 2,
        compiler_params=pltpu.CompilerParams(vmem_limit_bytes=32 * 1024 * 1024),
        name="attend_self",
    )(q, leaf_kv)


def merge_kernel(part, back_ref, codes_ref, own_ref, own_lse, *refs):
    out_ref, lse = refs[-2:]
    leaf = pl.program_id(0)

    @pl.when(leaf == 0)
    def _():
        for g in range(8):
            for z, t in enumerate((FIRST[g], SECOND[g])):
                code = codes_ref[t].astype(jnp.float32)
                value = code[0:LV] + code[LV:2 * LV] + code[2 * LV:3 * LV]
                for n in range(LV):
                    lse[z, n, g:g + 1] = value[n:n + 1]

    l0, l1, l2 = own_lse[leaf + part * LV], lse[0, leaf], lse[1, leaf]
    top = jnp.maximum(l0, jnp.maximum(l1, l2))
    w0, w1, w2 = jnp.exp(l0 - top), jnp.exp(l1 - top), jnp.exp(l2 - top)
    inv = 1.0 / (w0 + w1 + w2)
    eye = iota((R, 128), 0) == iota((R, 128), 1)

    def spread(w, g):
        return jnp.sum(jnp.where(eye, w[g:g + 1], 0.0), axis=1, keepdims=True)

    s0, s1, s2 = w0 * inv, w1 * inv, w2 * inv
    for g in range(8):
        o = (
            spread(s0, g) * own_ref[g]
            + spread(s1, g) * back_ref[FIRST[g]].astype(jnp.float32)
            + spread(s2, g) * back_ref[SECOND[g]].astype(jnp.float32)
        )
        for j in range(5):
            out_ref[:, (g * 5 + j) * 128:(g * 5 + j + 1) * 128] = o[j * 16:(j + 1) * 16]


def merge(part, back, own, own_lse, before):
    in_specs = [
        pl.BlockSpec((16, R, 128), lambda n: (0, n, 0)),
        pl.BlockSpec((16, CODES, 128), lambda n: (0, ROWS // CODES, 0)),
        pl.BlockSpec((8, R, 128), lambda n: (0, n + part * LV, 0)),
        pl.BlockSpec((8, 8, 128), lambda n: (0, 0, 0)),
    ]
    args = [back, back, own, own_lse]
    if before is not None:
        in_specs.append(pl.BlockSpec(memory_space=pl.ANY))
        args.append(before)
    return pl.pallas_call(
        functools.partial(merge_kernel, part),
        grid=(LV,),
        out_shape=jax.ShapeDtypeStruct((128, 5120), jnp.float32),
        in_specs=in_specs,
        out_specs=pl.BlockSpec((16, 5120), lambda n: (n + part * LV, 0)),
        scratch_shapes=[pltpu.VMEM((2, 8, 8, 128), jnp.float32)],
        input_output_aliases={} if before is None else {4: 0},
        compiler_params=pltpu.CompilerParams(vmem_limit_bytes=32 * 1024 * 1024),
        name="merge",
    )(*args)


NEAR = (0, 4, 5, 6, 7)
FAR = (1, 2, 3)


def shards(queries, leaf_kv, node_kv, node_lengths, ancestors):
    me = jnp.stack([lax.axis_index("node"), lax.axis_index("leaf") % 2]).astype(jnp.int32)
    outgoing = list(pack_queries(ancestors, queries))
    pieces = list(pack_kv(node_kv))

    def travel(i):
        return lax.ppermute(pieces[i], ("leaf", "node"), travel_pairs(i)) if i else pieces[0]

    def swap(x):
        return lax.all_to_all(x, "node", split_axis=0, concat_axis=0, tiled=True)

    arrived = [swap(outgoing[0])]
    near = [travel(i) for i in NEAR]
    rest = lax.optimization_barrier((*near, *(pieces[i] for i in FAR)))
    near, rest = list(rest[:len(NEAR)]), rest[len(NEAR):]
    for i, piece in zip(FAR, rest):
        pieces[i] = piece
    far = [travel(i) for i in FAR]
    state = attend(me, node_lengths, arrived[0], near, NEAR, None, False)
    state = list(state)
    state[0], state[1], *far = lax.optimization_barrier((*state, *far))
    outgoing[1], *far = lax.optimization_barrier((outgoing[1], *far))
    arrived.append(swap(outgoing[1]))
    answer = attend(me, node_lengths, arrived[0], far, FAR, state, True)
    own, own_lse = attend_self(queries, leaf_kv)
    out = merge(0, swap(answer), own, own_lse, None)
    answer = attend(me, node_lengths, arrived[1], near + far, NEAR + FAR, None, True)
    return merge(1, swap(answer), own, own_lse, out)


def solution(mesh):
    placed = (
        P(("leaf", "node"), None),
        P(None, ("leaf", "node"), None),
        P(None, ("leaf", "node"), None, None),
        P("leaf"),
        P(("leaf", "node"), None),
    )
    return jax.shard_map(
        shards, mesh=mesh, in_specs=placed, out_specs=P(("leaf", "node"), None), check_vma=False
    )
```

```python
import functools
import jax
import jax.numpy as jnp
from jax import lax
from jax.experimental import pallas as pl
from jax.experimental.pallas import tpu as pltpu
from jax.sharding import PartitionSpec as P

SCALE2 = (128 ** -0.5) * 1.4426950408889634
LN2 = 0.6931471805599453
SPAN = 1024
R = 80
SHIFTS = (
    ((0, 0), (0, 0)),
    ((2, 0), (0, 2)),
    ((1, 1), (3, 3)),
    ((3, 1), (1, 3)),
    ((0, 1), (0, 1)),
    ((0, 3), (0, 3)),
    ((1, 0), (1, 0)),
    ((3, 0), (3, 0)),
)
COLOUR = tuple((y % 2) * 4 + (x + 2 * (y // 2)) % 4 for y in range(4) for x in range(4))
FIRST = tuple(COLOUR.index(g) for g in range(8))
SECOND = tuple(15 - COLOUR[::-1].index(g) for g in range(8))
PARTS = 2
LV = 8 // PARTS
ROWS = LV * R
LEAVES = 16 * LV
TRASH = LEAVES
CODES = 4 * LV


SIZES = (512, 768, 1024)


def pick_size(length):
    size = SIZES[-1]
    for nk in SIZES[-2::-1]:
        size = jnp.where(length <= nk, nk, size)
    return size


def iota(shape, axis):
    return lax.broadcasted_iota(jnp.int32, shape, axis)


def rank_leaves(held, tail, meta, lists, sem):
    named = tail[0].astype(jnp.float32)
    for src in range(1, 16):
        named = named + tail[src].astype(jnp.float32)
    nodes = jnp.full((128, 128), -1, jnp.int32)
    for i, node in enumerate(held):
        nodes = jnp.where(iota((128, 128), 0) == i, node, nodes)
    nodes = nodes.astype(jnp.float32)
    member = (nodes == named[0:1]) | (nodes == named[1:2]) | (nodes == named[2:3])
    member = member & (iota((128, 128), 1) < LEAVES)
    member = jnp.where(member, 1.0, 0.0).astype(jnp.bfloat16)
    lower = jnp.where(iota((128, 128), 1) <= iota((128, 128), 0), 1.0, 0.0).astype(jnp.bfloat16)
    count = lax.dot_general(lower, member, (((1,), (1,)), ((), ())), preferred_element_type=jnp.float32)
    place = iota((128, 128), 1).astype(jnp.float32)
    for i in range(len(held)):
        before = jnp.where(count[:, i:i + 1] <= place, 1.0, 0.0)
        meta[i:i + 1] = jnp.sum(before, axis=0, keepdims=True).astype(jnp.int32)
    meta[8:9] = count[127:128].astype(jnp.int32)
    copy = pltpu.make_async_copy(meta, lists, sem)
    copy.start()
    copy.wait()


def attend_kernel(slots, C, U, first, last, me_ref, lengths, q_in, *refs):
    held = len(slots)
    kv_in, refs = refs[:held], refs[held:]
    if not first:
        state_in, refs = refs[:2], refs[2:]
    if last:
        out_ref, refs = refs[0], refs[1:]
    else:
        state_out, refs = refs[:2], refs[2:]
    (kv, acc, top, tot, sa, sb, meta, lists, seen, items, lens, sem, meta_sem, state_sem, *refs) = refs
    q_ref, tail, q_sem, *refs = refs
    tail_copy = pltpu.make_async_copy(q_in.at[:, ROWS:ROWS + 16], tail, q_sem.at[0])
    tail_copy.start()
    copies = [pltpu.make_async_copy(q_in.at[:, 0:ROWS], q_ref, q_sem.at[1])]
    for i in range(held):
        for z in range(2):
            copies.append(
                pltpu.make_async_copy(kv_in[i].at[z], kv.at[i, z], sem.at[i, z])
            )
    if not first:
        for z, (a, b) in enumerate(zip(state_in, (acc, top))):
            copies.append(pltpu.make_async_copy(a, b.at[0:LEAVES], state_sem.at[z]))
    for c in copies:
        c.start()
    me = me_ref[0]
    core = me_ref[1]
    nodes = []
    for i in slots:
        dy, dx = (jnp.where(core == 0, a, b) for a, b in zip(*SHIFTS[i]))
        nodes.append((me // 4 + 4 - dy) % 4 * 4 + (me % 4 + 4 - dx) % 4)
    for i in range(held):
        lens[i] = lengths[nodes[i]]

    def clear(i, _):
        seen[i] = 0
        return 0

    lax.fori_loop(0, LEAVES + 1, clear, 0)
    tail_copy.wait()
    rank_leaves(nodes, tail, meta, lists, meta_sem)

    bounds = []
    cursor = jnp.int32(0)
    for nk in SIZES:
        start = cursor

        def node(i, cur):
            n = jnp.where(pick_size(lens[i]) == nk, lists[8, i], 0)

            def some(k, cur):
                items[0, cur] = i
                for z in range(C):
                    leaf = lists[i, jnp.minimum(C * k + z, n - 1)]
                    dest = jnp.where(C * k + z < n, leaf, TRASH)
                    items[1 + z, cur] = leaf + dest * 256 + seen[dest] * 65536
                    seen[dest] = 1
                return cur + 1

            return lax.fori_loop(0, (n + C - 1) // C, some, cur)

        cursor = lax.fori_loop(0, held, node, start)
        short = (start - cursor) % U

        def pad(k, _):
            items[0, cursor + k] = items[0, cursor - 1]
            for z in range(C):
                items[1 + z, cursor + k] = items[1 + z, cursor - 1] % 256 + TRASH * 256
            return 0

        lax.fori_loop(0, short, pad, 0)
        cursor = cursor + short
        bounds.append((start, cursor))

    for c in copies:
        c.wait()

    def scores(t, nk):
        leaves = [items[1 + z, t] % 256 for z in range(C)]
        q = jnp.concatenate(
            [q_ref[n // LV, pl.ds(pl.multiple_of(n % LV * R, 16), R)] for n in leaves], axis=0
        )
        return lax.dot_general(
            q, kv[items[0, t], 0, :nk], (((1,), (1,)), ((), ())), preferred_element_type=jnp.float32
        )

    def soften(s_ref, t, nk):
        i = items[0, t]
        sure = SIZES[SIZES.index(nk) - 1] if nk != SIZES[0] else 0
        keep = iota((1, nk - sure), 1) + sure < lens[i]
        s = jnp.where(keep, s_ref[:, sure:nk], -1e30)
        if sure:
            s = jnp.concatenate([s_ref[:, :sure], s], axis=1)
        m = jnp.max(s, axis=1, keepdims=True)
        p = jnp.exp2((s - m) * SCALE2).astype(jnp.bfloat16)
        v = jnp.concatenate([kv[i, 1, :nk], jnp.ones((nk, 128), jnp.bfloat16)], axis=1)
        o = jnp.dot(p, v, preferred_element_type=jnp.float32)
        m = jnp.broadcast_to(m * SCALE2, (C * R, 128))
        for z in range(C):
            code = items[1 + z, t]
            at = code // 256 % 256
            old = code >= 65536
            mz = m[z * R:(z + 1) * R]
            oz = o[z * R:(z + 1) * R]
            if first:
                m0 = jnp.where(old, top[at], -1e30)
                w0 = jnp.where(old, tot[at], 0.0)
                a0 = jnp.where(old, acc[at], 0.0)
            else:
                m0 = top[at]
                w0 = jnp.where(old, tot[at], 1.0)
                a0 = acc[at]
            mn = jnp.maximum(m0, mz)
            e0 = jnp.exp2(m0 - mn)
            e1 = jnp.exp2(mz - mn)
            top[at] = mn
            tot[at] = w0 * e0 + oz[:, 128:256] * e1
            acc[at] = a0 * e0 + oz[:, 0:128] * e1

    for nk, (start, end) in zip(SIZES, bounds):

        @pl.when(end > start)
        def _():
            sa[:, :nk] = scores(start, nk)

            def step(u, _):
                t = start + U * u
                for z in range(U):
                    now, then = (sa, sb) if z % 2 == 0 else (sb, sa)
                    then[:, :nk] = scores(jnp.minimum(t + z + 1, end - 1), nk)
                    soften(now, t + z, nk)
                return 0

            lax.fori_loop(0, (end - start) // U, step, 0)

    def load(n):
        old = seen[n] == 1
        if first:
            return (
                jnp.where(old, acc[n], 0.0),
                jnp.where(old, top[n], -1e30),
                jnp.where(old, tot[n], 1.0),
            )
        return acc[n], top[n], jnp.where(old, tot[n], 1.0)

    if not last:

        def even(i, _):
            for z in range(4):
                n = i * 4 + z
                a, m, w = load(n)
                acc[n] = a / w
                top[n] = m + jnp.log2(w)
            return 0

        lax.fori_loop(0, LEAVES // 4, even, 0)
        copies = [
            pltpu.make_async_copy(a.at[0:LEAVES], b, state_sem.at[z])
            for z, (a, b) in enumerate(zip((acc, top), state_out))
        ]
        for c in copies:
            c.start()
        for c in copies:
            c.wait()
        return

    out_buf, out_sem = refs
    eye = iota((R, 128), 0) == iota((R, 128), 1)

    def pick(x):
        return jnp.sum(jnp.where(eye, x, 0.0), axis=0, keepdims=True)

    def finish(dev, _):
        tops, tots = [], []
        for n in range(LV):
            a, m, w = load(dev * LV + n)
            out_buf[dev, n * R:(n + 1) * R] = (a / w).astype(jnp.bfloat16)
            tops.append(pick(m))
            tots.append(pick(w))
        used = iota((LV, 128), 1) < R
        tots = jnp.where(used, jnp.concatenate(tots, axis=0), 1.0)
        value = jnp.concatenate(tops, axis=0) * LN2 + jnp.log(tots)
        hi = value.astype(jnp.bfloat16).astype(jnp.float32)
        mid = (value - hi).astype(jnp.bfloat16).astype(jnp.float32)
        lo = value - hi - mid
        codes = jnp.concatenate([hi, mid, lo, jnp.zeros_like(lo)], axis=0)
        out_buf[dev, ROWS:ROWS + CODES] = codes.astype(jnp.bfloat16)
        pltpu.make_async_copy(out_buf.at[dev], out_ref.at[dev], out_sem.at[dev]).start()
        return 0

    lax.fori_loop(0, 16, finish, 0)
    for dev in range(16):
        pltpu.make_async_copy(out_buf.at[dev], out_ref.at[dev], out_sem.at[dev]).wait()


def attend(me, lengths, q, kvs, slots, state, last, C, U):
    smem = pl.BlockSpec(memory_space=pltpu.SMEM)
    hbm = pl.BlockSpec(memory_space=pl.ANY)
    f32 = jnp.float32
    first = state is None
    held = len(slots)
    if last:
        out_shape, out_specs = jax.ShapeDtypeStruct((16, ROWS + CODES, 128), jnp.bfloat16), hbm
    else:
        out_shape, out_specs = (jax.ShapeDtypeStruct((LEAVES, R, 128), f32),) * 2, (hbm,) * 2
    extra = () if first else state
    scratch = [
        pltpu.VMEM((held, 2, SPAN, 128), jnp.bfloat16),
        pltpu.VMEM((LEAVES + 1, R, 128), f32),
        pltpu.VMEM((LEAVES + 1, R, 128), f32),
        pltpu.VMEM((LEAVES + 1, R, 128), f32),
        pltpu.VMEM((C * R, SPAN), f32),
        pltpu.VMEM((C * R, SPAN), f32),
        pltpu.VMEM((16, 128), jnp.int32),
        pltpu.SMEM((16, 128), jnp.int32),
        pltpu.SMEM((LEAVES + 1,), jnp.int32),
        pltpu.SMEM((1 + C, 256), jnp.int32),
        pltpu.SMEM((8,), jnp.int32),
        pltpu.SemaphoreType.DMA((held, 2)),
        pltpu.SemaphoreType.DMA,
        pltpu.SemaphoreType.DMA((2,)),
        pltpu.VMEM((16, ROWS, 128), jnp.bfloat16),
        pltpu.VMEM((16, 16, 128), jnp.bfloat16),
        pltpu.SemaphoreType.DMA((2,)),
    ]
    if last:
        scratch += [pltpu.VMEM((16, ROWS + CODES, 128), jnp.bfloat16), pltpu.SemaphoreType.DMA((16,))]
    return pl.pallas_call(
        functools.partial(attend_kernel, slots, C, U, first, last),
        out_shape=out_shape,
        in_specs=[smem] * 2 + [hbm] * (1 + held + len(extra)),
        out_specs=out_specs,
        scratch_shapes=scratch,
        compiler_params=pltpu.CompilerParams(vmem_limit_bytes=62 * 1024 * 1024),
        cost_estimate=pl.CostEstimate(
            flops=held * 2_000_000_000, bytes_accessed=held * 2_000_000, transcendentals=held * 1_000_000
        ),
        name="attend" if last else "attend_near",
    )(me, lengths, q, *kvs, *extra)


def travel_pairs(i):
    pairs = []
    for tree in range(8):
        dy, dx = SHIFTS[i][tree % 2]
        for y in range(4):
            for x in range(4):
                pairs.append((tree * 16 + y * 4 + x, tree * 16 + (y + dy) % 4 * 4 + (x + dx) % 4))
    return pairs


def colour_of(y, x):
    return (y % 2) * 4 + (x + 2 * (y // 2)) % 4


def pack_queries_kernel(anc, q_ref, *refs):
    outs, (buf, sem) = refs[:PARTS], refs[PARTS:]
    me = lax.axis_index("node")
    lane = iota((16, 128), 1)
    row = iota((16, 128), 0)
    copies = []
    for part in range(PARTS):
        named = jnp.zeros((16, 128), jnp.int32)
        for n in range(LV):
            for d in range(3):
                named = jnp.where((row == d) & (lane == me * LV + n), anc[part * LV + n, d], named)
        named = named.astype(jnp.float32).astype(jnp.bfloat16)
        for g in range(8):
            for n in range(LV):
                for j in range(5):
                    at = n * R + j * 16
                    head = g * 5 + j
                    tok = (part * LV + n) * 16
                    buf[part, g, at:at + 16] = q_ref[tok:tok + 16, head * 128:(head + 1) * 128]
            buf[part, g, ROWS:ROWS + 16] = named
            for t in (FIRST[g], SECOND[g]):
                copies.append(pltpu.make_async_copy(buf.at[part, g], outs[part].at[t], sem.at[part, t]))
                copies[-1].start()
    for c in copies:
        c.wait()


def pack_queries(anc, q):
    hbm = pl.BlockSpec(memory_space=pl.ANY)
    return pl.pallas_call(
        pack_queries_kernel,
        out_shape=(jax.ShapeDtypeStruct((16, ROWS + 16, 128), jnp.bfloat16),) * PARTS,
        in_specs=[pl.BlockSpec(memory_space=pltpu.SMEM), pl.BlockSpec(memory_space=pltpu.VMEM)],
        out_specs=(hbm,) * PARTS,
        scratch_shapes=[
            pltpu.VMEM((PARTS, 8, ROWS + 16, 128), jnp.bfloat16),
            pltpu.SemaphoreType.DMA((PARTS, 16)),
        ],
        compiler_params=pltpu.CompilerParams(vmem_limit_bytes=16 * 1024 * 1024),
        name="pack_queries",
    )(anc, q)


def pack_kv_kernel(slots, kv_ref, *refs):
    outs, (buf, sem) = refs[:len(slots)], refs[len(slots):]
    me = lax.axis_index("node")
    y, x = me // 4, me % 4
    core = lax.axis_index("leaf") % 2
    loads, stores = [], []
    for n, i in enumerate(slots):
        dy, dx = (jnp.where(core == 0, a, b) for a, b in zip(*SHIFTS[i]))
        at = pl.multiple_of(colour_of((y + dy) % 4, (x + dx) % 4) * 128, 128)
        for z in range(2):
            loads.append(
                pltpu.make_async_copy(kv_ref.at[z, 0, :, pl.ds(at, 128)], buf.at[n, z], sem.at[0, n, z])
            )
            stores.append(pltpu.make_async_copy(buf.at[n, z], outs[n].at[z], sem.at[1, n, z]))
    for c in loads:
        c.start()
    for c, d in zip(loads, stores):
        c.wait()
        d.start()
    for d in stores:
        d.wait()


def pack_kv(kv, slots):
    hbm = pl.BlockSpec(memory_space=pl.ANY)
    held = len(slots)
    return pl.pallas_call(
        functools.partial(pack_kv_kernel, slots),
        out_shape=tuple(jax.ShapeDtypeStruct((2, SPAN, 128), jnp.bfloat16) for _ in slots),
        in_specs=[hbm],
        out_specs=(hbm,) * held,
        scratch_shapes=[
            pltpu.VMEM((held, 2, SPAN, 128), jnp.bfloat16),
            pltpu.SemaphoreType.DMA((2, held, 2)),
        ],
        compiler_params=pltpu.CompilerParams(vmem_limit_bytes=16 * 1024 * 1024),
        name="pack_kv",
    )(kv)


def self_kernel(q_ref, kv_ref, *refs):
    outs, lse_ref = refs[:PARTS], refs[PARTS]
    row = lax.broadcasted_iota(jnp.int32, (640, 128), 0)
    col = lax.broadcasted_iota(jnp.int32, (640, 128), 1)
    keep = (row // R == col // 16) & (col % 16 <= row % 16)
    eye = lax.broadcasted_iota(jnp.int32, (R, 128), 0) == lax.broadcasted_iota(jnp.int32, (R, 128), 1)
    for g in range(8):
        q = jnp.concatenate(
            [
                q_ref[n * 16:(n + 1) * 16, (g * 5 + j) * 128:(g * 5 + j + 1) * 128]
                for n in range(8)
                for j in range(5)
            ],
            axis=0,
        )
        k = kv_ref[0, :, g * 128:(g + 1) * 128]
        v = kv_ref[1, :, g * 128:(g + 1) * 128]
        s = lax.dot_general(q, k, (((1,), (1,)), ((), ())), preferred_element_type=jnp.float32)
        s = jnp.where(keep, s, -1e30)
        m = jnp.max(s, axis=1, keepdims=True)
        p = jnp.exp2((s - m) * SCALE2)
        l = jnp.sum(p, axis=1, keepdims=True)
        o = jnp.dot(p.astype(jnp.bfloat16), v, preferred_element_type=jnp.float32)
        o = o / l
        for part in range(PARTS):
            outs[part][g] = o[part * ROWS:(part + 1) * ROWS]
        value = jnp.broadcast_to(m * (SCALE2 * LN2) + jnp.log(l), (640, 128))
        for n in range(8):
            part = jnp.where(eye, value[n * R:(n + 1) * R], 0.0)
            lse_ref[n, g:g + 1] = jnp.sum(part, axis=0, keepdims=True)


def attend_self(q, leaf_kv):
    vmem = pl.BlockSpec(memory_space=pltpu.VMEM)
    return pl.pallas_call(
        self_kernel,
        out_shape=(jax.ShapeDtypeStruct((8, ROWS, 128), jnp.float32),) * PARTS
        + (jax.ShapeDtypeStruct((8, 8, 128), jnp.float32),),
        in_specs=[vmem] * 2,
        out_specs=(vmem,) * (PARTS + 1),
        compiler_params=pltpu.CompilerParams(vmem_limit_bytes=32 * 1024 * 1024),
        name="attend_self",
    )(q, leaf_kv)


def merge_kernel(part, back_ref, codes_ref, own_ref, own_lse, *refs):
    out_ref, lse = refs[-2:]
    leaf = pl.program_id(0)

    @pl.when(leaf == 0)
    def _():
        for g in range(8):
            for z, t in enumerate((FIRST[g], SECOND[g])):
                code = codes_ref[t].astype(jnp.float32)
                value = code[0:LV] + code[LV:2 * LV] + code[2 * LV:3 * LV]
                for n in range(LV):
                    lse[z, n, g:g + 1] = value[n:n + 1]

    l0, l1, l2 = own_lse[leaf + part * LV], lse[0, leaf], lse[1, leaf]
    top = jnp.maximum(l0, jnp.maximum(l1, l2))
    w0, w1, w2 = jnp.exp(l0 - top), jnp.exp(l1 - top), jnp.exp(l2 - top)
    inv = 1.0 / (w0 + w1 + w2)
    eye = iota((R, 128), 0) == iota((R, 128), 1)

    def spread(w, g):
        return jnp.sum(jnp.where(eye, w[g:g + 1], 0.0), axis=1, keepdims=True)

    s0, s1, s2 = w0 * inv, w1 * inv, w2 * inv
    for g in range(8):
        o = (
            spread(s0, g) * own_ref[g]
            + spread(s1, g) * back_ref[FIRST[g]].astype(jnp.float32)
            + spread(s2, g) * back_ref[SECOND[g]].astype(jnp.float32)
        )
        for j in range(5):
            out_ref[:, (g * 5 + j) * 128:(g * 5 + j + 1) * 128] = o[j * 16:(j + 1) * 16]


def merge(part, back, own, own_lse, before):
    in_specs = [
        pl.BlockSpec((16, R, 128), lambda n: (0, n, 0)),
        pl.BlockSpec((16, CODES, 128), lambda n: (0, ROWS // CODES, 0)),
        pl.BlockSpec((8, R, 128), lambda n: (0, n, 0)),
        pl.BlockSpec((8, 8, 128), lambda n: (0, 0, 0)),
    ]
    args = [back, back, own, own_lse]
    if before is not None:
        in_specs.append(pl.BlockSpec(memory_space=pl.ANY))
        args.append(before)
    return pl.pallas_call(
        functools.partial(merge_kernel, part),
        grid=(LV,),
        out_shape=jax.ShapeDtypeStruct((128, 5120), jnp.float32),
        in_specs=in_specs,
        out_specs=pl.BlockSpec((16, 5120), lambda n: (n + part * LV, 0)),
        scratch_shapes=[pltpu.VMEM((2, 8, 8, 128), jnp.float32)],
        input_output_aliases={} if before is None else {4: 0},
        compiler_params=pltpu.CompilerParams(vmem_limit_bytes=32 * 1024 * 1024),
        name="merge",
    )(*args)


NEAR = (4, 5, 6, 7)
FAR = (1, 2, 3)


def shards(queries, leaf_kv, node_kv, node_lengths, ancestors):
    me = jnp.stack([lax.axis_index("node"), lax.axis_index("leaf") % 2]).astype(jnp.int32)
    sent = list(pack_kv(node_kv, NEAR))
    loose = queries
    outgoing = list(pack_queries(ancestors, loose))
    kept, *later = pack_kv(node_kv, (0,) + FAR)

    def travel(piece, i):
        return lax.ppermute(piece, ("leaf", "node"), travel_pairs(i))

    def swap(x):
        return lax.all_to_all(x, "node", split_axis=0, concat_axis=0, tiled=True)

    arrived = [swap(outgoing[0])]
    near = [travel(piece, i) for piece, i in zip(sent, NEAR)]
    near[2], near[3], *later = lax.optimization_barrier((near[2], near[3], *later))
    near = [kept, *near]
    far = [travel(piece, i) for piece, i in zip(later, FAR)]
    held = (0,) + NEAR
    state = attend(me, node_lengths, arrived[0], near, held, None, False, 4, 2)
    done = lax.optimization_barrier((*state, *far))
    state, far = done[:2], done[2:]
    outgoing[1], *far = lax.optimization_barrier((outgoing[1], *far))
    arrived.append(swap(outgoing[1]))
    answer = attend(me, node_lengths, arrived[0], far, FAR, state, True, 4, 2)
    *own, own_lse = attend_self(queries, leaf_kv)
    out = merge(0, swap(answer), own[0], own_lse, None)
    answer = attend(me, node_lengths, arrived[1], near + far, held + FAR, None, True, 4, 2)
    return merge(1, swap(answer), own[1], own_lse, out)


def solution(mesh):
    placed = (
        P(("leaf", "node"), None),
        P(None, ("leaf", "node"), None),
        P(None, ("leaf", "node"), None, None),
        P("leaf"),
        P(("leaf", "node"), None),
    )
    return jax.shard_map(
        shards, mesh=mesh, in_specs=placed, out_specs=P(("leaf", "node"), None), check_vma=False
    )
```

```python
import functools
import jax
import jax.numpy as jnp
from jax import lax
from jax.experimental import pallas as pl
from jax.experimental.pallas import tpu as pltpu
from jax.sharding import PartitionSpec as P

SCALE2 = (128 ** -0.5) * 1.4426950408889634
LN2 = 0.6931471805599453
SPAN = 1024
R = 80
SHIFTS = (
    ((0, 0), (0, 0)),
    ((2, 0), (0, 2)),
    ((1, 1), (3, 3)),
    ((3, 1), (1, 3)),
    ((0, 1), (0, 1)),
    ((0, 3), (0, 3)),
    ((1, 0), (1, 0)),
    ((3, 0), (3, 0)),
)
COLOUR = tuple((y % 2) * 4 + (x + 2 * (y // 2)) % 4 for y in range(4) for x in range(4))
FIRST = tuple(COLOUR.index(g) for g in range(8))
SECOND = tuple(15 - COLOUR[::-1].index(g) for g in range(8))
PARTS = 2
LV = 8 // PARTS
ROWS = LV * R
LEAVES = 16 * LV
TRASH = LEAVES
CODES = 4 * LV


SIZES = (512, 768, 1024)


def pick_size(length):
    size = SIZES[-1]
    for nk in SIZES[-2::-1]:
        size = jnp.where(length <= nk, nk, size)
    return size


def iota(shape, axis):
    return lax.broadcasted_iota(jnp.int32, shape, axis)


def rank_leaves(held, tail, meta, lists, sem):
    named = tail[0].astype(jnp.float32)
    for src in range(1, 16):
        named = named + tail[src].astype(jnp.float32)
    nodes = jnp.full((128, 128), -1, jnp.int32)
    for i, node in enumerate(held):
        nodes = jnp.where(iota((128, 128), 0) == i, node, nodes)
    nodes = nodes.astype(jnp.float32)
    member = (nodes == named[0:1]) | (nodes == named[1:2]) | (nodes == named[2:3])
    member = member & (iota((128, 128), 1) < LEAVES)
    member = jnp.where(member, 1.0, 0.0).astype(jnp.bfloat16)
    lower = jnp.where(iota((128, 128), 1) <= iota((128, 128), 0), 1.0, 0.0).astype(jnp.bfloat16)
    count = lax.dot_general(lower, member, (((1,), (1,)), ((), ())), preferred_element_type=jnp.float32)
    place = iota((128, 128), 1).astype(jnp.float32)
    for i in range(len(held)):
        before = jnp.where(count[:, i:i + 1] <= place, 1.0, 0.0)
        meta[i:i + 1] = jnp.sum(before, axis=0, keepdims=True).astype(jnp.int32)
    meta[8:9] = count[127:128].astype(jnp.int32)
    copy = pltpu.make_async_copy(meta, lists, sem)
    copy.start()
    copy.wait()


def attend_kernel(slots, C, U, first, last, me_ref, lengths, q_in, *refs):
    held = len(slots)
    kv_in, refs = refs[:held], refs[held:]
    if not first:
        state_in, refs = refs[:2], refs[2:]
    if last:
        out_ref, refs = refs[0], refs[1:]
    else:
        state_out, refs = refs[:2], refs[2:]
    (kv, acc, top, tot, sa, sb, meta, lists, seen, items, lens, sem, meta_sem, state_sem, *refs) = refs
    q_ref, tail, q_sem, *refs = refs
    tail_copy = pltpu.make_async_copy(q_in.at[:, ROWS:ROWS + 16], tail, q_sem.at[0])
    tail_copy.start()
    copies = [pltpu.make_async_copy(q_in.at[:, 0:ROWS], q_ref, q_sem.at[1])]
    for i in range(held):
        for z in range(2):
            copies.append(
                pltpu.make_async_copy(kv_in[i].at[z], kv.at[i, z], sem.at[i, z])
            )
    if not first:
        for z, (a, b) in enumerate(zip(state_in, (acc, top))):
            copies.append(pltpu.make_async_copy(a, b.at[0:LEAVES], state_sem.at[z]))
    for c in copies:
        c.start()
    me = me_ref[0]
    core = me_ref[1]
    nodes = []
    for i in slots:
        dy, dx = (jnp.where(core == 0, a, b) for a, b in zip(*SHIFTS[i]))
        nodes.append((me // 4 + 4 - dy) % 4 * 4 + (me % 4 + 4 - dx) % 4)
    for i in range(held):
        lens[i] = lengths[nodes[i]]

    def clear(i, _):
        seen[i] = 0
        return 0

    lax.fori_loop(0, LEAVES + 1, clear, 0)
    tail_copy.wait()
    rank_leaves(nodes, tail, meta, lists, meta_sem)

    bounds = []
    cursor = jnp.int32(0)
    for nk in SIZES:
        start = cursor

        def node(i, cur):
            n = jnp.where(pick_size(lens[i]) == nk, lists[8, i], 0)

            def some(k, cur):
                items[0, cur] = i
                for z in range(C):
                    leaf = lists[i, jnp.minimum(C * k + z, n - 1)]
                    dest = jnp.where(C * k + z < n, leaf, TRASH)
                    items[1 + z, cur] = leaf + dest * 256 + seen[dest] * 65536
                    seen[dest] = 1
                return cur + 1

            return lax.fori_loop(0, (n + C - 1) // C, some, cur)

        cursor = lax.fori_loop(0, held, node, start)
        short = (start - cursor) % U

        def pad(k, _):
            items[0, cursor + k] = items[0, cursor - 1]
            for z in range(C):
                items[1 + z, cursor + k] = items[1 + z, cursor - 1] % 256 + TRASH * 256
            return 0

        lax.fori_loop(0, short, pad, 0)
        cursor = cursor + short
        bounds.append((start, cursor))

    for c in copies:
        c.wait()

    def scores(t, nk):
        leaves = [items[1 + z, t] % 256 for z in range(C)]
        q = jnp.concatenate(
            [q_ref[n // LV, pl.ds(pl.multiple_of(n % LV * R, 16), R)] for n in leaves], axis=0
        )
        return lax.dot_general(
            q, kv[items[0, t], 0, :nk], (((1,), (1,)), ((), ())), preferred_element_type=jnp.float32
        )

    def soften(s_ref, t, nk):
        i = items[0, t]
        sure = SIZES[SIZES.index(nk) - 1] if nk != SIZES[0] else 0
        keep = iota((1, nk - sure), 1) + sure < lens[i]
        s = jnp.where(keep, s_ref[:, sure:nk], -1e30)
        if sure:
            s = jnp.concatenate([s_ref[:, :sure], s], axis=1)
        m = jnp.max(s, axis=1, keepdims=True)
        p = jnp.exp2((s - m) * SCALE2).astype(jnp.bfloat16)
        v = jnp.concatenate([kv[i, 1, :nk], jnp.ones((nk, 128), jnp.bfloat16)], axis=1)
        o = jnp.dot(p, v, preferred_element_type=jnp.float32)
        m = jnp.broadcast_to(m * SCALE2, (C * R, 128))
        for z in range(C):
            code = items[1 + z, t]
            at = code // 256 % 256
            old = code >= 65536
            mz = m[z * R:(z + 1) * R]
            oz = o[z * R:(z + 1) * R]
            if first:
                m0 = jnp.where(old, top[at], -1e30)
                w0 = jnp.where(old, tot[at], 0.0)
                a0 = jnp.where(old, acc[at], 0.0)
            else:
                m0 = top[at]
                w0 = jnp.where(old, tot[at], 1.0)
                a0 = acc[at]
            mn = jnp.maximum(m0, mz)
            e0 = jnp.exp2(m0 - mn)
            e1 = jnp.exp2(mz - mn)
            top[at] = mn
            tot[at] = w0 * e0 + oz[:, 128:256] * e1
            acc[at] = a0 * e0 + oz[:, 0:128] * e1

    for nk, (start, end) in zip(SIZES, bounds):

        @pl.when(end > start)
        def _():
            sa[:, :nk] = scores(start, nk)

            def step(u, _):
                t = start + U * u
                for z in range(U):
                    now, then = (sa, sb) if z % 2 == 0 else (sb, sa)
                    then[:, :nk] = scores(jnp.minimum(t + z + 1, end - 1), nk)
                    soften(now, t + z, nk)
                return 0

            lax.fori_loop(0, (end - start) // U, step, 0)

    def load(n):
        old = seen[n] == 1
        if first:
            return (
                jnp.where(old, acc[n], 0.0),
                jnp.where(old, top[n], -1e30),
                jnp.where(old, tot[n], 1.0),
            )
        return acc[n], top[n], jnp.where(old, tot[n], 1.0)

    if not last:

        def even(i, _):
            for z in range(4):
                n = i * 4 + z
                a, m, w = load(n)
                acc[n] = a / w
                top[n] = m + jnp.log2(w)
            return 0

        lax.fori_loop(0, LEAVES // 4, even, 0)
        copies = [
            pltpu.make_async_copy(a.at[0:LEAVES], b, state_sem.at[z])
            for z, (a, b) in enumerate(zip((acc, top), state_out))
        ]
        for c in copies:
            c.start()
        for c in copies:
            c.wait()
        return

    out_buf, out_sem = refs
    eye = iota((R, 128), 0) == iota((R, 128), 1)

    def pick(x):
        return jnp.sum(jnp.where(eye, x, 0.0), axis=0, keepdims=True)

    def finish(dev, _):
        tops, tots = [], []
        for n in range(LV):
            a, m, w = load(dev * LV + n)
            out_buf[dev, n * R:(n + 1) * R] = (a / w).astype(jnp.bfloat16)
            tops.append(pick(m))
            tots.append(pick(w))
        used = iota((LV, 128), 1) < R
        tots = jnp.where(used, jnp.concatenate(tots, axis=0), 1.0)
        value = jnp.concatenate(tops, axis=0) * LN2 + jnp.log(tots)
        hi = value.astype(jnp.bfloat16).astype(jnp.float32)
        mid = (value - hi).astype(jnp.bfloat16).astype(jnp.float32)
        lo = value - hi - mid
        codes = jnp.concatenate([hi, mid, lo, jnp.zeros_like(lo)], axis=0)
        out_buf[dev, ROWS:ROWS + CODES] = codes.astype(jnp.bfloat16)
        pltpu.make_async_copy(out_buf.at[dev], out_ref.at[dev], out_sem.at[dev]).start()
        return 0

    lax.fori_loop(0, 16, finish, 0)
    for dev in range(16):
        pltpu.make_async_copy(out_buf.at[dev], out_ref.at[dev], out_sem.at[dev]).wait()


def attend(me, lengths, q, kvs, slots, state, last, C, U):
    smem = pl.BlockSpec(memory_space=pltpu.SMEM)
    hbm = pl.BlockSpec(memory_space=pl.ANY)
    f32 = jnp.float32
    first = state is None
    held = len(slots)
    if last:
        out_shape, out_specs = jax.ShapeDtypeStruct((16, ROWS + CODES, 128), jnp.bfloat16), hbm
    else:
        out_shape, out_specs = (jax.ShapeDtypeStruct((LEAVES, R, 128), f32),) * 2, (hbm,) * 2
    extra = () if first else state
    scratch = [
        pltpu.VMEM((held, 2, SPAN, 128), jnp.bfloat16),
        pltpu.VMEM((LEAVES + 1, R, 128), f32),
        pltpu.VMEM((LEAVES + 1, R, 128), f32),
        pltpu.VMEM((LEAVES + 1, R, 128), f32),
        pltpu.VMEM((C * R, SPAN), f32),
        pltpu.VMEM((C * R, SPAN), f32),
        pltpu.VMEM((16, 128), jnp.int32),
        pltpu.SMEM((16, 128), jnp.int32),
        pltpu.SMEM((LEAVES + 1,), jnp.int32),
        pltpu.SMEM((1 + C, 256), jnp.int32),
        pltpu.SMEM((8,), jnp.int32),
        pltpu.SemaphoreType.DMA((held, 2)),
        pltpu.SemaphoreType.DMA,
        pltpu.SemaphoreType.DMA((2,)),
        pltpu.VMEM((16, ROWS, 128), jnp.bfloat16),
        pltpu.VMEM((16, 16, 128), jnp.bfloat16),
        pltpu.SemaphoreType.DMA((2,)),
    ]
    if last:
        scratch += [pltpu.VMEM((16, ROWS + CODES, 128), jnp.bfloat16), pltpu.SemaphoreType.DMA((16,))]
    return pl.pallas_call(
        functools.partial(attend_kernel, slots, C, U, first, last),
        out_shape=out_shape,
        in_specs=[smem] * 2 + [hbm] * (1 + held + len(extra)),
        out_specs=out_specs,
        scratch_shapes=scratch,
        compiler_params=pltpu.CompilerParams(vmem_limit_bytes=(60 if first and last else 62) * 1024 * 1024),
        cost_estimate=pl.CostEstimate(
            flops=held * 2_000_000_000, bytes_accessed=held * 2_000_000, transcendentals=held * 1_000_000
        ),
        name="attend" if last else "attend_near",
    )(me, lengths, q, *kvs, *extra)


def travel_pairs(i):
    pairs = []
    for tree in range(8):
        dy, dx = SHIFTS[i][tree % 2]
        for y in range(4):
            for x in range(4):
                pairs.append((tree * 16 + y * 4 + x, tree * 16 + (y + dy) % 4 * 4 + (x + dx) % 4))
    return pairs


def colour_of(y, x):
    return (y % 2) * 4 + (x + 2 * (y // 2)) % 4


def pack_queries_kernel(anc, q_ref, *refs):
    outs, (buf, sem) = refs[:PARTS], refs[PARTS:]
    me = lax.axis_index("node")
    lane = iota((16, 128), 1)
    row = iota((16, 128), 0)
    copies = []
    for part in range(PARTS):
        named = jnp.zeros((16, 128), jnp.int32)
        for n in range(LV):
            for d in range(3):
                named = jnp.where((row == d) & (lane == me * LV + n), anc[part * LV + n, d], named)
        named = named.astype(jnp.float32).astype(jnp.bfloat16)
        for g in range(8):
            for n in range(LV):
                for j in range(5):
                    at = n * R + j * 16
                    head = g * 5 + j
                    tok = (part * LV + n) * 16
                    buf[part, g, at:at + 16] = q_ref[tok:tok + 16, head * 128:(head + 1) * 128]
            buf[part, g, ROWS:ROWS + 16] = named
            for t in (FIRST[g], SECOND[g]):
                copies.append(pltpu.make_async_copy(buf.at[part, g], outs[part].at[t], sem.at[part, t]))
                copies[-1].start()
    for c in copies:
        c.wait()


def pack_queries(anc, q):
    hbm = pl.BlockSpec(memory_space=pl.ANY)
    return pl.pallas_call(
        pack_queries_kernel,
        out_shape=(jax.ShapeDtypeStruct((16, ROWS + 16, 128), jnp.bfloat16),) * PARTS,
        in_specs=[pl.BlockSpec(memory_space=pltpu.SMEM), pl.BlockSpec(memory_space=pltpu.VMEM)],
        out_specs=(hbm,) * PARTS,
        scratch_shapes=[
            pltpu.VMEM((PARTS, 8, ROWS + 16, 128), jnp.bfloat16),
            pltpu.SemaphoreType.DMA((PARTS, 16)),
        ],
        compiler_params=pltpu.CompilerParams(vmem_limit_bytes=16 * 1024 * 1024),
        name="pack_queries",
    )(anc, q)


def pack_kv_kernel(slots, kv_ref, *refs):
    outs, (buf, sem) = refs[:len(slots)], refs[len(slots):]
    me = lax.axis_index("node")
    y, x = me // 4, me % 4
    core = lax.axis_index("leaf") % 2
    loads, stores = [], []
    for n, i in enumerate(slots):
        dy, dx = (jnp.where(core == 0, a, b) for a, b in zip(*SHIFTS[i]))
        at = pl.multiple_of(colour_of((y + dy) % 4, (x + dx) % 4) * 128, 128)
        for z in range(2):
            loads.append(
                pltpu.make_async_copy(kv_ref.at[z, 0, :, pl.ds(at, 128)], buf.at[n, z], sem.at[0, n, z])
            )
            stores.append(pltpu.make_async_copy(buf.at[n, z], outs[n].at[z], sem.at[1, n, z]))
    for c in loads:
        c.start()
    for c, d in zip(loads, stores):
        c.wait()
        d.start()
    for d in stores:
        d.wait()


def pack_kv(kv, slots):
    hbm = pl.BlockSpec(memory_space=pl.ANY)
    held = len(slots)
    return pl.pallas_call(
        functools.partial(pack_kv_kernel, slots),
        out_shape=tuple(jax.ShapeDtypeStruct((2, SPAN, 128), jnp.bfloat16) for _ in slots),
        in_specs=[hbm],
        out_specs=(hbm,) * held,
        scratch_shapes=[
            pltpu.VMEM((held, 2, SPAN, 128), jnp.bfloat16),
            pltpu.SemaphoreType.DMA((2, held, 2)),
        ],
        compiler_params=pltpu.CompilerParams(vmem_limit_bytes=16 * 1024 * 1024),
        name="pack_kv",
    )(kv)


def self_kernel(q_ref, kv_ref, *refs):
    outs, lse_ref = refs[:PARTS], refs[PARTS]
    row = lax.broadcasted_iota(jnp.int32, (640, 128), 0)
    col = lax.broadcasted_iota(jnp.int32, (640, 128), 1)
    keep = (row // R == col // 16) & (col % 16 <= row % 16)
    eye = lax.broadcasted_iota(jnp.int32, (R, 128), 0) == lax.broadcasted_iota(jnp.int32, (R, 128), 1)
    for g in range(8):
        q = jnp.concatenate(
            [
                q_ref[n * 16:(n + 1) * 16, (g * 5 + j) * 128:(g * 5 + j + 1) * 128]
                for n in range(8)
                for j in range(5)
            ],
            axis=0,
        )
        k = kv_ref[0, :, g * 128:(g + 1) * 128]
        v = kv_ref[1, :, g * 128:(g + 1) * 128]
        s = lax.dot_general(q, k, (((1,), (1,)), ((), ())), preferred_element_type=jnp.float32)
        s = jnp.where(keep, s, -1e30)
        m = jnp.max(s, axis=1, keepdims=True)
        p = jnp.exp2((s - m) * SCALE2)
        l = jnp.sum(p, axis=1, keepdims=True)
        o = jnp.dot(p.astype(jnp.bfloat16), v, preferred_element_type=jnp.float32)
        o = o / l
        for part in range(PARTS):
            outs[part][g] = o[part * ROWS:(part + 1) * ROWS]
        value = jnp.broadcast_to(m * (SCALE2 * LN2) + jnp.log(l), (640, 128))
        for n in range(8):
            part = jnp.where(eye, value[n * R:(n + 1) * R], 0.0)
            lse_ref[n, g:g + 1] = jnp.sum(part, axis=0, keepdims=True)


def attend_self(q, leaf_kv):
    vmem = pl.BlockSpec(memory_space=pltpu.VMEM)
    return pl.pallas_call(
        self_kernel,
        out_shape=(jax.ShapeDtypeStruct((8, ROWS, 128), jnp.float32),) * PARTS
        + (jax.ShapeDtypeStruct((8, 8, 128), jnp.float32),),
        in_specs=[vmem] * 2,
        out_specs=(vmem,) * (PARTS + 1),
        compiler_params=pltpu.CompilerParams(vmem_limit_bytes=32 * 1024 * 1024),
        name="attend_self",
    )(q, leaf_kv)


def merge_kernel(part, back_ref, codes_ref, own_ref, own_lse, *refs):
    out_ref, lse = refs[-2:]
    leaf = pl.program_id(0)

    @pl.when(leaf == 0)
    def _():
        for g in range(8):
            for z, t in enumerate((FIRST[g], SECOND[g])):
                code = codes_ref[t].astype(jnp.float32)
                value = code[0:LV] + code[LV:2 * LV] + code[2 * LV:3 * LV]
                for n in range(LV):
                    lse[z, n, g:g + 1] = value[n:n + 1]

    l0, l1, l2 = own_lse[leaf + part * LV], lse[0, leaf], lse[1, leaf]
    top = jnp.maximum(l0, jnp.maximum(l1, l2))
    w0, w1, w2 = jnp.exp(l0 - top), jnp.exp(l1 - top), jnp.exp(l2 - top)
    inv = 1.0 / (w0 + w1 + w2)
    eye = iota((R, 128), 0) == iota((R, 128), 1)

    def spread(w, g):
        return jnp.sum(jnp.where(eye, w[g:g + 1], 0.0), axis=1, keepdims=True)

    s0, s1, s2 = w0 * inv, w1 * inv, w2 * inv
    for g in range(8):
        o = (
            spread(s0, g) * own_ref[g]
            + spread(s1, g) * back_ref[FIRST[g]].astype(jnp.float32)
            + spread(s2, g) * back_ref[SECOND[g]].astype(jnp.float32)
        )
        for j in range(5):
            out_ref[:, (g * 5 + j) * 128:(g * 5 + j + 1) * 128] = o[j * 16:(j + 1) * 16]


def merge(part, back, own, own_lse, before):
    in_specs = [
        pl.BlockSpec((16, R, 128), lambda n: (0, n, 0)),
        pl.BlockSpec((16, CODES, 128), lambda n: (0, ROWS // CODES, 0)),
        pl.BlockSpec((8, R, 128), lambda n: (0, n, 0)),
        pl.BlockSpec((8, 8, 128), lambda n: (0, 0, 0)),
    ]
    args = [back, back, own, own_lse]
    if before is not None:
        in_specs.append(pl.BlockSpec(memory_space=pl.ANY))
        args.append(before)
    return pl.pallas_call(
        functools.partial(merge_kernel, part),
        grid=(LV,),
        out_shape=jax.ShapeDtypeStruct((128, 5120), jnp.float32),
        in_specs=in_specs,
        out_specs=pl.BlockSpec((16, 5120), lambda n: (n + part * LV, 0)),
        scratch_shapes=[pltpu.VMEM((2, 8, 8, 128), jnp.float32)],
        input_output_aliases={} if before is None else {4: 0},
        compiler_params=pltpu.CompilerParams(vmem_limit_bytes=32 * 1024 * 1024),
        name="merge",
    )(*args)


NEAR = (4, 5, 6, 7)
FAR = (1, 2, 3)


def shards(queries, leaf_kv, node_kv, node_lengths, ancestors):
    me = jnp.stack([lax.axis_index("node"), lax.axis_index("leaf") % 2]).astype(jnp.int32)
    sent = list(pack_kv(node_kv, NEAR))
    loose = queries
    outgoing = list(pack_queries(ancestors, loose))
    kept, *later = pack_kv(node_kv, (0,) + FAR)

    def travel(piece, i):
        return lax.ppermute(piece, ("leaf", "node"), travel_pairs(i))

    def swap(x):
        return lax.all_to_all(x, "node", split_axis=0, concat_axis=0, tiled=True)

    arrived = [swap(outgoing[0])]
    near = [travel(piece, i) for piece, i in zip(sent, NEAR)]
    near[2], near[3], *later = lax.optimization_barrier((near[2], near[3], *later))
    near = [kept, *near]
    far = [travel(piece, i) for piece, i in zip(later, FAR)]
    held = (0,) + NEAR
    state = attend(me, node_lengths, arrived[0], near, held, None, False, 4, 2)
    done = lax.optimization_barrier((*state, *far))
    state, far = done[:2], done[2:]
    outgoing[1], *far = lax.optimization_barrier((outgoing[1], *far))
    arrived.append(swap(outgoing[1]))
    answer = attend(me, node_lengths, arrived[0], far, FAR, state, True, 4, 2)
    *own, own_lse = attend_self(queries, leaf_kv)
    out = merge(0, swap(answer), own[0], own_lse, None)
    answer = attend(me, node_lengths, arrived[1], near + far, held + FAR, None, True, 4, 2)
    return merge(1, swap(answer), own[1], own_lse, out)


def solution(mesh):
    placed = (
        P(("leaf", "node"), None),
        P(None, ("leaf", "node"), None),
        P(None, ("leaf", "node"), None, None),
        P("leaf"),
        P(("leaf", "node"), None),
    )
    return jax.shard_map(
        shards, mesh=mesh, in_specs=placed, out_specs=P(("leaf", "node"), None), check_vma=False
    )
```
